128 devices in a mesh: section: 4 (over z), dp: 8 (over x, y_lo), tensor: 4 (over y_hi, core).
Axes of the slice: x: 4, y: 4 (y_hi: 2, y_lo: 2; y = y_hi * 2 + y_lo), z: 4, core: 2. Of those that a mesh axis runs over, the one named last changes fastest.
Arguments:
- base: bfloat16 [4, 256, 8192], P(None, None, 'dp'), may hold values from -6 to 6
- w_in: bfloat16 [4, 8192, 14336], P('section', 'dp', 'tensor'), may hold values from -0.0625 to 0.0625
- w_out: bfloat16 [4, 14336, 8192], P('section', 'tensor', 'dp'), may hold values from -0.046875 to 0.046875
- basis: float32 [8192, 128], P('dp'), may hold values from -0.0625 to 0.0625
- cotangent: float32 [4, 256, 128], P(None, 'dp'), may hold values from -6 to 6
Outputs:
- coefs: float32 [4, 4, 256, 128], P('section', None, 'dp')
- grads: float32 [4, 4, 256, 128], P('section', None, 'dp')
- grad_up: bfloat16 [4, 8192, 14336], P('section', 'dp', 'tensor')
- down_coefs: float32 [4, 14336, 128], P('section', 'tensor')
The draws below stay inside these ranges and needn't reach their ends.
All inputs are finite; a program needn't handle non-finite values.
Results may differ from the reference program's by a relative error of at most 0.007.
Values may be sent and summed in bfloat16 or wider, within the bound.
No kernel may reach another device: no remote copies, remote signals or barrier semaphores. Data moves between devices by JAX's collectives and lax.ppermute only.
A program may use at most 128 MiB of HBM per device.

```python
import jax
import jax.numpy as jnp
from jax import lax

D = 8192
HID = 14336
R = 128
MB = 4
SECTIONS = 4
TOKENS = 256


def level_of(own_key, shape, shards, smallest, high):
    level, own = 1.0, jax.random.fold_in(own_key, 6)
    for position, shards_of in shards:
        draws = jnp.exp(jax.random.uniform(jax.random.fold_in(own, position), (shards_of,), jnp.float32, smallest / len(shards), high / len(shards)))
        level = level * jnp.repeat(draws, shape[position] // shards_of).reshape([-1 if axis == position else 1 for axis in range(len(shape))])
    return level


def bell_draw(rng, shape, width, reach, cuts=(), dtype=jnp.bfloat16):
    level = level_of(rng, shape, cuts, -0.22, 0.18) if cuts else 1.0
    entries = jax.random.normal(rng, shape, jnp.float32) * width * level
    return jnp.minimum(jnp.maximum(entries, -reach), reach).astype(dtype)


def setup_inputs(seed: int = 0) -> dict:
    arg_keys = jax.random.split(jax.random.key(seed), 6)
    return {
        "base": bell_draw(arg_keys[0], (MB, TOKENS, D), 1.0, 6.0, ((2, 8),)),
        "w_in": bell_draw(arg_keys[1], (SECTIONS, D, HID), D ** -0.5, 0.0625, ((0, 4), (1, 8), (2, 4))),
        "w_out": bell_draw(arg_keys[2], (SECTIONS, HID, D), HID ** -0.5, 0.046875, ((0, 4), (1, 4), (2, 8))),
        "basis": bell_draw(arg_keys[3], (D, R), D ** -0.5, 0.0625, ((0, 8),), jnp.float32),
        "cotangent": bell_draw(arg_keys[4], (MB, TOKENS, R), 1.0, 6.0, ((1, 8),), jnp.float32),
    }


def silu_slope(pre_act):
    sigmoid_val = jax.nn.sigmoid(pre_act)
    return sigmoid_val * (1.0 + pre_act * (1.0 - sigmoid_val))


def reference(base, w_in, w_out, basis, cotangent):
    highest = lax.Precision.HIGHEST
    gram_matrix = jnp.dot(basis.T, basis, precision=highest)
    carried = jnp.zeros((MB, TOKENS, R), jnp.float32)
    coef_list = []
    saved_inputs = []
    saved_pres = []
    ups = []
    downs = []
    for section_idx in range(SECTIONS):
        proj_up = jnp.dot(w_in[section_idx].astype(jnp.float32).T, basis, precision=highest)
        proj_down = jnp.dot(w_out[section_idx].astype(jnp.float32), basis, precision=highest).astype(jnp.bfloat16)
        ups.append(proj_up)
        downs.append(proj_down)
        section_inputs = []
        section_pres = []
        outputs = []
        for micro_idx in range(MB):
            c_in = carried[micro_idx]
            rebuilt = jnp.dot(c_in, basis.T, precision=highest)
            section_input = (base[micro_idx].astype(jnp.float32) + rebuilt).astype(jnp.bfloat16)
            pre_act = jnp.dot(section_input, w_in[section_idx], preferred_element_type=jnp.float32)
            hidden = jax.nn.silu(pre_act).astype(jnp.bfloat16)
            coef_next = jnp.dot(c_in, gram_matrix, precision=highest) + jnp.dot(hidden, proj_down, preferred_element_type=jnp.float32)
            section_inputs.append(section_input)
            section_pres.append(pre_act)
            outputs.append(coef_next)
        carried = jnp.stack(outputs)
        coef_list.append(carried)
        saved_inputs.append(section_inputs)
        saved_pres.append(section_pres)
    grad_list = [None] * SECTIONS
    up_list = [None] * SECTIONS
    down_list = [None] * SECTIONS
    upstream = cotangent
    for section_idx in range(SECTIONS - 1, -1, -1):
        down_wide = lax.optimization_barrier(downs[section_idx]).astype(jnp.float32)
        g_ins = []
        totals = jnp.zeros((HID, R), jnp.float32)
        accumulated = jnp.zeros((D, HID), jnp.float32)
        for micro_idx in range(MB):
            g_out = upstream[micro_idx]
            pre_act = saved_pres[section_idx][micro_idx]
            g_hidden = jnp.dot(g_out, down_wide.T, precision=highest)
            g_pre = g_hidden * silu_slope(pre_act)
            g_in = jnp.dot(g_out, gram_matrix, precision=highest) + jnp.dot(g_pre, ups[section_idx], precision=highest)
            g_ins.append(g_in)
            accumulated = accumulated + jnp.dot(saved_inputs[section_idx][micro_idx].T, g_pre.astype(jnp.bfloat16), preferred_element_type=jnp.float32)
            hidden_wide = lax.optimization_barrier(jax.nn.silu(pre_act).astype(jnp.bfloat16)).astype(jnp.float32)
            totals = totals + jnp.dot(hidden_wide.T, g_out, precision=highest)
        up_list[section_idx] = accumulated.astype(jnp.bfloat16)
        down_list[section_idx] = totals
        upstream = jnp.stack(g_ins)
        grad_list[section_idx] = upstream
    return jnp.stack(coef_list), jnp.stack(grad_list), jnp.stack(up_list), jnp.stack(down_list)
```

```python
import jax
import jax.numpy as jnp
from jax import lax
from jax.experimental import pallas as pl
from jax.experimental.pallas import tpu as pltpu
from jax.sharding import PartitionSpec as P

BF = jnp.bfloat16
F32 = jnp.float32
HIGHEST = lax.Precision.HIGHEST
NT = (((1,), (1,)), ((), ()))
CHUNK = 512


def split2(x):
    hi = x.astype(BF)
    return hi, (x - hi.astype(F32)).astype(BF)


def mm(a, b):
    return jnp.dot(a, b, preferred_element_type=F32)


def mm_nt(a, b):
    return lax.dot_general(a, b, NT, preferred_element_type=F32)


def sigma(v):
    return 0.5 * jnp.tanh(0.5 * v) + 0.5


def wide(x):
    hi, lo = split2(x)
    return jnp.concatenate([hi, lo], axis=1)


def twice(x):
    return jnp.concatenate([x, x], axis=0)


def chunks_of(width):
    return [slice(i, i + CHUNK) for i in range(0, width, CHUNK)]


def gram_share(x, gram):
    return 0.25 * jnp.dot(x, gram, precision=HIGHEST, preferred_element_type=F32)


def forward_kernel(base_ref, up_ref, down_ref, gram_ref, r0, r1, r2, r3, part_ref):
    c = (r0[...] + r1[...]) + (r2[...] + r3[...])
    cw = wide(c)
    acc = gram_share(c, gram_ref[...])
    for cols in chunks_of(base_ref.shape[1]):
        pre = base_ref[:, cols] + mm(cw, twice(up_ref[:, cols]))
        hidden = (pre * sigma(pre)).astype(BF)
        acc += mm_nt(hidden, down_ref[:, cols])
    part_ref[...] = acc


def first_kernel(base_ref, down_ref, part_ref):
    acc = jnp.zeros(part_ref.shape, F32)
    for cols in chunks_of(base_ref.shape[1]):
        pre = base_ref[:, cols]
        hidden = (pre * sigma(pre)).astype(BF)
        acc += mm_nt(hidden, down_ref[:, cols])
    part_ref[...] = acc


def middle_kernel(
    base_ref, up_ref, down_ref, gram_ref, r0, r1, r2, r3, c_ref, part_ref, hidden_ref, slope_ref
):
    c = (r0[...] + r1[...]) + (r2[...] + r3[...])
    c_ref[...] = c
    cw = wide(c)
    acc = gram_share(c, gram_ref[...])
    for cols in chunks_of(base_ref.shape[1]):
        pre = base_ref[:, cols] + mm(cw, twice(up_ref[:, cols]))
        sig = sigma(pre)
        hidden = (pre * sig).astype(BF)
        hidden_ref[:, cols] = hidden
        slope_ref[:, cols] = sig * (1.0 + pre * (1.0 - sig))
        acc += mm_nt(hidden, down_ref[:, cols])
    part_ref[...] = acc


def backward_kernel(slope_ref, up_ref, down_ref, gram_ref, g_ref, part_ref):
    g = g_ref[...]
    gw = wide(g)
    acc = gram_share(g, gram_ref[...])
    for cols in chunks_of(slope_ref.shape[1]):
        g_pre = mm(gw, twice(down_ref[:, cols])) * slope_ref[:, cols]
        hi, lo = split2(g_pre)
        acc += mm_nt(hi, up_ref[:, cols]) + mm_nt(lo, up_ref[:, cols])
    part_ref[...] = acc


def last_kernel(slope_ref, hidden_ref, up_ref, down_ref, gram_ref, g_ref, part_ref, g_pre_ref, dc_ref):
    g = g_ref[...]
    gw = wide(g)
    gt = wide(g.T)
    acc = gram_share(g, gram_ref[...])
    for cols in chunks_of(slope_ref.shape[1]):
        g_pre = mm(gw, twice(down_ref[:, cols])) * slope_ref[:, cols]
        hi, lo = split2(g_pre)
        g_pre_ref[:, cols] = hi
        dc_ref[:, cols] = mm(gt, twice(hidden_ref[:, cols])).astype(BF)
        acc += mm_nt(hi, up_ref[:, cols]) + mm_nt(lo, up_ref[:, cols])
    part_ref[...] = acc


def call(kernel, outs, *args):
    return pl.pallas_call(
        kernel,
        out_shape=outs,
        compiler_params=pltpu.CompilerParams(vmem_limit_bytes=40 * 1024 * 1024),
    )(*args)


def relay(x, by, k, sections, tensors):
    pairs = [
        (s * tensors + t, (s + by) * tensors + (t ^ k))
        for s in range(sections)
        for t in range(tensors)
        if 0 <= s + by < sections
    ]
    return lax.ppermute(x, ("section", "tensor"), pairs)


def tensor_sum(x, tensors):
    parts = [x] + [
        lax.ppermute(x, "tensor", [(t, t ^ k) for t in range(tensors)]) for k in range(1, tensors)
    ]
    return (parts[0] + parts[1]) + (parts[2] + parts[3])


def swap(x):
    return lax.all_to_all(x, "dp", 0, 0, tiled=True)


def spread(x, count):
    return swap(jnp.broadcast_to(x[None], (count,) + x.shape))


def on_device(base, w_in, w_out, basis, cotangent):
    sections = lax.axis_size("section")
    tensors = lax.axis_size("tensor")
    dp = lax.axis_size("dp")
    is_last = lax.axis_index("section") == sections - 1
    micro, tokens, width = base.shape
    rows = tokens // dp
    own = micro * rows
    rank = basis.shape[1]
    w_in = w_in[0]
    w_out = w_out[0]
    hid = w_in.shape[1]
    tok = jax.ShapeDtypeStruct((own, rank), F32)
    wide_bf = jax.ShapeDtypeStruct((own, hid), BF)
    wide_f = jax.ShapeDtypeStruct((own, hid), F32)

    base_rows = base.reshape(micro, dp, rows, width).transpose(1, 0, 2, 3).reshape(dp * own, width)
    basis_t = wide(basis).T
    gram = lax.psum(
        lax.dot_general(basis, basis, (((0,), (0,)), ((), ())), precision=HIGHEST), "dp"
    )
    up2 = mm(basis_t, w_in)
    down2 = mm_nt(basis_t, w_out)
    proj = jnp.concatenate(
        [
            (up2[:rank] + up2[rank:]).astype(BF).reshape(dp, rank // dp, hid),
            (down2[:rank] + down2[rank:]).astype(BF).reshape(dp, rank // dp, hid),
        ],
        axis=1,
    )
    proj = jnp.sum(swap(proj).reshape(dp, 2 * rank // dp, hid).astype(F32), axis=0).astype(BF)
    proj = spread(proj, dp).reshape(dp, 2, rank // dp, hid)
    up = proj[:, 0].reshape(rank, hid)
    down = proj[:, 1].reshape(rank, hid)
    base_part = mm(base_rows, w_in).astype(BF).reshape(dp, own, hid)
    base_pre = jnp.sum(swap(base_part).astype(F32), axis=0)

    part = call(first_kernel, tok, base_pre, down)
    for turn in range(1, sections - 1):
        got = [relay(part, 1, k, sections, tensors) for k in range(tensors)]
        part = call(forward_kernel, tok, base_pre, up, down, gram, *got)
    got = [relay(part, 1, k, sections, tensors) for k in range(tensors)]
    c_in, part, hidden, slope = call(
        middle_kernel, (tok, tok, wide_bf, wide_f), base_pre, up, down, gram, *got
    )
    coefs = tensor_sum(part, tensors)
    c_all = spread(c_in.astype(BF), dp).reshape(dp * own, rank)

    cot = cotangent.reshape(own, rank)
    g_out = cot
    for turn in range(sections - 1):
        part = call(backward_kernel, tok, slope, up, down, gram, g_out)
        got = [relay(part, -1, k, sections, tensors) for k in range(tensors)]
        g_out = jnp.where(is_last, cot, (got[0] + got[1]) + (got[2] + got[3]))
    part, g_pre, dc = call(
        last_kernel, (tok, wide_bf, jax.ShapeDtypeStruct((rank, hid), BF)),
        slope, hidden, up, down, gram, g_out,
    )
    grads = tensor_sum(part, tensors)

    dc = jnp.sum(swap(dc.reshape(dp, rank // dp, hid)).astype(F32), axis=0).astype(BF)
    dc = spread(dc, dp).reshape(rank, hid)
    g_all = spread(g_pre, dp).reshape(dp * own, hid)
    inputs = (base_rows.astype(F32) + mm_nt(c_all, basis.astype(BF))).astype(BF)
    grad_up = lax.dot_general(
        inputs, g_all, (((0,), (0,)), ((), ())), preferred_element_type=F32
    ).astype(BF)
    return (
        coefs.reshape(1, micro, rows, rank),
        grads.reshape(1, micro, rows, rank),
        grad_up[None],
        dc.T.astype(F32)[None],
    )


def solution(mesh):
    return jax.shard_map(
        on_device,
        mesh=mesh,
        in_specs=(
            P(None, None, "dp"),
            P("section", "dp", "tensor"),
            P("section", "tensor", "dp"),
            P("dp", None),
            P(None, "dp", None),
        ),
        out_specs=(
            P("section", None, "dp", None),
            P("section", None, "dp", None),
            P("section", "dp", "tensor"),
            P("section", "tensor", None),
        ),
        check_vma=False,
    )
```

```python
import jax
import jax.numpy as jnp
from jax import lax
from jax.experimental import pallas as pl
from jax.experimental.pallas import tpu as pltpu
from jax.sharding import PartitionSpec as P

BF = jnp.bfloat16
F32 = jnp.float32
HIGHEST = lax.Precision.HIGHEST
NT = (((1,), (1,)), ((), ()))
CHUNK = 512
X_SIZE = 4
RELATIVE = ((0, 0), (0, 1), (-1, 0), (-1, 1), (1, 0), (1, 1), (2, 0), (2, 1))
PARAMS = pltpu.CompilerParams(vmem_limit_bytes=48 * 1024 * 1024)


def split2(x):
    hi = x.astype(BF)
    return hi, (x - hi.astype(F32)).astype(BF)


def mm(a, b):
    return jnp.dot(a, b, preferred_element_type=F32)


def mm_nt(a, b):
    return lax.dot_general(a, b, NT, preferred_element_type=F32)


def sigma(v):
    return 0.5 * jnp.tanh(0.5 * v) + 0.5


def wide(x):
    return jnp.concatenate(split2(x), axis=1)


def tall(x):
    return jnp.concatenate(split2(x), axis=0)


def twice(x):
    return jnp.concatenate([x, x], axis=0)


def chunks_of(width):
    return [slice(i, i + CHUNK) for i in range(0, width, CHUNK)]


def gram_share(x, gram):
    return 0.25 * jnp.dot(x, gram, precision=HIGHEST, preferred_element_type=F32)


def first_kernel(base_ref, down_ref, part_ref):
    acc = jnp.zeros(part_ref.shape, F32)
    for cols in chunks_of(base_ref.shape[1]):
        pre = base_ref[:, cols]
        hidden = (pre * sigma(pre)).astype(BF)
        acc += mm_nt(hidden, down_ref[:, cols])
    part_ref[...] = acc


def forward_kernel(base_ref, up_ref, down_ref, gram_ref, r0, r1, part_ref):
    c = r0[...] + r1[...]
    cw = wide(c)
    acc = gram_share(c, gram_ref[...])
    for cols in chunks_of(base_ref.shape[1]):
        pre = base_ref[:, cols] + mm(cw, twice(up_ref[:, cols]))
        hidden = (pre * sigma(pre)).astype(BF)
        acc += mm_nt(hidden, down_ref[:, cols])
    part_ref[...] = acc


def middle_kernel(base_ref, up_ref, down_ref, gram_ref, r0, r1, c_ref, part_ref, slope_ref):
    c = r0[...] + r1[...]
    c_ref[...] = c.astype(BF)
    cw = wide(c)
    acc = gram_share(c, gram_ref[...])
    for cols in chunks_of(base_ref.shape[1]):
        pre = base_ref[:, cols] + mm(cw, twice(up_ref[:, cols]))
        sig = sigma(pre)
        hidden = (pre * sig).astype(BF)
        slope_ref[:, cols] = sig * (1.0 + pre * (1.0 - sig))
        acc += mm_nt(hidden, down_ref[:, cols])
    part_ref[...] = acc


def backward_kernel(last_ref, slope_ref, up_ref, down_ref, gram_ref, cot_ref, r0, r1, g_ref, part_ref):
    g = jnp.where(last_ref[0] == 1, cot_ref[...], r0[...] + r1[...])
    g_ref[...] = g
    gw = wide(g)
    acc = gram_share(g, gram_ref[...])
    for cols in chunks_of(slope_ref.shape[1]):
        g_pre = mm(gw, twice(down_ref[:, cols])) * slope_ref[:, cols]
        hi, lo = split2(g_pre)
        acc += mm_nt(hi, up_ref[:, cols]) + mm_nt(lo, up_ref[:, cols])
    part_ref[...] = acc


def call(kernel, outs, *args):
    return pl.pallas_call(kernel, out_shape=outs, compiler_params=PARAMS)(*args)


def proj_kernel(place_ref, basis_ref, w_in_ref, w_out_ref, *refs):
    outs, (basis_t, both) = refs[:-2], refs[-2:]
    rank = basis_ref.shape[1]
    rows = rank // len(RELATIVE)

    @pl.when(pl.program_id(0) == 0)
    def _():
        basis_t[...] = tall(basis_ref[...].T)

    up = mm(basis_t[...], w_in_ref[...])
    down = mm_nt(basis_t[...], w_out_ref[...])
    both[:rank] = up[:rank] + up[rank:]
    both[rank:] = down[:rank] + down[rank:]
    for j, out in enumerate(outs):
        start = pl.multiple_of(place_ref[j] * rows, rows)
        out[:rows] = both[pl.ds(start, rows)].astype(BF)
        out[rows:] = both[pl.ds(rank + start, rows)].astype(BF)


def project(place, basis, w_in, w_out):
    width, rank = basis.shape
    hid = w_in.shape[1]
    rows = 2 * rank // len(RELATIVE)
    count = len(RELATIVE)
    return pl.pallas_call(
        proj_kernel,
        out_shape=[jax.ShapeDtypeStruct((rows, hid), BF)] * count,
        grid_spec=pltpu.PrefetchScalarGridSpec(
            num_scalar_prefetch=1,
            grid=(hid // CHUNK,),
            in_specs=[
                pl.BlockSpec((width, rank), lambda i, p: (0, 0)),
                pl.BlockSpec((width, CHUNK), lambda i, p: (0, i)),
                pl.BlockSpec((CHUNK, width), lambda i, p: (i, 0)),
            ],
            out_specs=[pl.BlockSpec((rows, CHUNK), lambda i, p: (0, i))] * count,
            scratch_shapes=[pltpu.VMEM((2 * rank, width), BF), pltpu.VMEM((2 * rank, CHUNK), F32)],
        ),
        compiler_params=PARAMS,
    )(place, basis, w_in, w_out)


def base_specs(base, dp):
    micro, tokens, width = base.shape
    return [
        pl.BlockSpec((micro, tokens // dp, width), lambda i, p, j=j: (0, p[j], 0))
        for j in range(len(RELATIVE))
    ]


def product_kernel(place_ref, *refs):
    count = len(RELATIVE)
    bases, w_ref, outs = refs[:count], refs[count], refs[count + 1 :]
    own = bases[0].shape[0] * bases[0].shape[1]
    for j in range(0, count, 2):
        rows = jnp.concatenate([b[...].reshape(own, b.shape[2]) for b in bases[j : j + 2]], axis=0)
        res = mm(rows, w_ref[...]).astype(BF)
        outs[j][...] = res[:own]
        outs[j + 1][...] = res[own:]


def product(place, base, w_in, dp):
    micro, tokens, width = base.shape
    hid = w_in.shape[1]
    own = micro * tokens // dp
    count = len(RELATIVE)
    return pl.pallas_call(
        product_kernel,
        out_shape=[jax.ShapeDtypeStruct((own, hid), BF)] * count,
        grid_spec=pltpu.PrefetchScalarGridSpec(
            num_scalar_prefetch=1,
            grid=(hid // CHUNK,),
            in_specs=base_specs(base, dp) + [pl.BlockSpec((width, CHUNK), lambda i, p: (0, i))],
            out_specs=[pl.BlockSpec((own, CHUNK), lambda i, p: (0, i))] * count,
        ),
        compiler_params=PARAMS,
    )(place, *([base] * count), w_in)


def assemble_kernel(place_ref, *refs):
    pieces, (up_ref, down_ref) = refs[:-2], refs[-2:]
    rows = up_ref.shape[1]
    flat = jnp.concatenate([p[...] for p in pieces], axis=0)
    for j in range(len(RELATIVE)):
        up_ref[place_ref[j]] = flat[2 * j * rows : (2 * j + 1) * rows]
        down_ref[place_ref[j]] = flat[(2 * j + 1) * rows : (2 * j + 2) * rows]


def assemble(place, pieces, rank, hid):
    count = len(RELATIVE)
    shape = (count, rank // count, hid)
    up, down = pl.pallas_call(
        assemble_kernel,
        out_shape=[jax.ShapeDtypeStruct(shape, BF)] * 2,
        grid_spec=pltpu.PrefetchScalarGridSpec(
            num_scalar_prefetch=1,
            grid=(hid // CHUNK,),
            in_specs=[pl.BlockSpec((p.shape[0], CHUNK), lambda i, p: (0, i)) for p in pieces],
            out_specs=[pl.BlockSpec((count, rank // count, CHUNK), lambda i, p: (0, 0, i))] * 2,
        ),
        compiler_params=PARAMS,
    )(place, *pieces)
    return up.reshape(rank, hid), down.reshape(rank, hid)


def prepare_kernel(place_ref, *refs):
    count = len(RELATIVE)
    bases, refs = refs[:count], refs[count:]
    basis_ref, c_refs, up_ref, pieces = refs[0], refs[1:5], refs[5], refs[6:-3]
    xt_ref, hidden_ref, slope_ref = refs[-3:]
    own = bases[0].shape[0] * bases[0].shape[1]

    @pl.when(pl.program_id(0) == 0)
    def _():
        basis = basis_ref[...].astype(BF)
        for j, b in enumerate(bases):
            c = c_refs[j // 2][(j % 2) * own : (j % 2 + 1) * own]
            x = b[...].reshape(own, b.shape[2]).astype(F32) + mm_nt(c, basis)
            xt_ref[:, j * own : (j + 1) * own] = x.T.astype(BF)

    up = up_ref[...]
    base_pre = jnp.concatenate([p[...] for p in pieces], axis=0)
    for j in range(count):
        rows = slice(j * own, (j + 1) * own)
        c = c_refs[j // 2][(j % 2) * own : (j % 2 + 1) * own]
        pre = base_pre[rows].astype(F32) + mm(c, up)
        sig = sigma(pre)
        hidden_ref[rows] = (pre * sig).astype(BF)
        slope_ref[rows] = (sig * (1.0 + pre * (1.0 - sig))).astype(BF)


def prepare(place, base, dp, basis, c_pieces, up, pieces):
    micro, tokens, width = base.shape
    hid = up.shape[1]
    every = micro * tokens
    whole = lambda a: pl.BlockSpec(a.shape, lambda i, p: (0, 0))
    column = lambda rows: pl.BlockSpec((rows, CHUNK), lambda i, p: (0, i))
    return pl.pallas_call(
        prepare_kernel,
        out_shape=[
            jax.ShapeDtypeStruct((width, every), BF),
            jax.ShapeDtypeStruct((every, hid), BF),
            jax.ShapeDtypeStruct((every, hid), BF),
        ],
        grid_spec=pltpu.PrefetchScalarGridSpec(
            num_scalar_prefetch=1,
            grid=(hid // CHUNK,),
            in_specs=base_specs(base, dp)
            + [whole(basis)]
            + [whole(c) for c in c_pieces]
            + [column(up.shape[0])]
            + [column(p.shape[0]) for p in pieces],
            out_specs=[
                pl.BlockSpec((width, every), lambda i, p: (0, 0)),
                column(every),
                column(every),
            ],
        ),
        compiler_params=PARAMS,
    )(place, *([base] * len(RELATIVE)), basis, *c_pieces, up, *pieces)


def finish_kernel(place_ref, g_ref, down_ref, xt_ref, hidden_ref, slope_ref, grad_ref, dc_ref, gw, gt):
    rank = down_ref.shape[0]
    own = g_ref.shape[1]

    @pl.when(pl.program_id(0) == 0)
    def _():
        for j in range(len(RELATIVE)):
            g = g_ref[place_ref[j]]
            gw[j * own : (j + 1) * own] = wide(g)
            gt[:, j * own : (j + 1) * own] = tall(g.T)

    g_pre = mm(gw[...], twice(down_ref[...])) * slope_ref[...].astype(F32)
    grad_ref[...] = mm(xt_ref[...], g_pre.astype(BF)).astype(BF)
    dc = mm(gt[...], hidden_ref[...])
    dc_ref[...] = (dc[:rank] + dc[rank:]).T


def finish(place, g_all, down, xt, hidden, slope):
    rank, hid = down.shape
    width, every = xt.shape
    column = lambda rows: pl.BlockSpec((rows, CHUNK), lambda i, p: (0, i))
    return pl.pallas_call(
        finish_kernel,
        out_shape=[jax.ShapeDtypeStruct((width, hid), BF), jax.ShapeDtypeStruct((hid, rank), F32)],
        grid_spec=pltpu.PrefetchScalarGridSpec(
            num_scalar_prefetch=1,
            grid=(hid // CHUNK,),
            in_specs=[
                pl.BlockSpec(g_all.shape, lambda i, p: (0, 0, 0)),
                column(rank),
                pl.BlockSpec(xt.shape, lambda i, p: (0, 0)),
                column(every),
                column(every),
            ],
            out_specs=[column(width), pl.BlockSpec((CHUNK, rank), lambda i, p: (i, 0))],
            scratch_shapes=[pltpu.VMEM((every, 2 * rank), BF), pltpu.VMEM((2 * rank, every), BF)],
        ),
        compiler_params=PARAMS,
    )(place, g_all, down, xt, hidden, slope)


def to_dp(x, dx, dy):
    size = lax.axis_size("dp")
    pairs = [(i, ((i // 2 + dx) % X_SIZE) * 2 + ((i % 2) ^ dy)) for i in range(size)]
    return lax.ppermute(x, "dp", pairs)


def to_tensor(x, k):
    size = lax.axis_size("tensor")
    return lax.ppermute(x, "tensor", [(t, t ^ k) for t in range(size)])


def hop(part, by):
    sections, tensors = lax.axis_size("section"), lax.axis_size("tensor")
    pair_sum = part + to_tensor(part, 1)
    pairs = [
        (s * tensors + t, (s + by) * tensors + (t ^ (2 * (t % 2))))
        for s in range(sections)
        for t in range(tensors)
        if 0 <= s + by < sections
    ]
    got = lax.ppermute(pair_sum, ("section", "tensor"), pairs)
    return got, to_tensor(got, 1)


def cat(*xs):
    return jnp.concatenate(xs, axis=0)


def plus(x, *ys):
    total = x.astype(F32)
    for start, y in ys:
        pads = ((start, x.shape[0] - start - y.shape[0]), (0, 0))
        total = total + jnp.pad(y.astype(F32), pads)
    return total.astype(x.dtype)


def reduce_blocks(blocks):
    b = dict(zip(RELATIVE, blocks))
    n = blocks[0].shape[0]
    h, q = n // 2, n // 4
    far = b[2, 1]
    u0, u1, v = to_dp(far[:q], 1, 0), to_dp(far[q:h], -1, 0), to_dp(far[h:], 0, 1)
    up = to_dp(cat(b[2, 0][:h], plus(b[1, 1][:h], (0, u0))), 1, 0)
    down = to_dp(cat(plus(b[2, 0][h:], (0, v)), plus(b[-1, 1][:h], (q, u1))), -1, 0)
    side = to_dp(cat(b[1, 1][h:], b[-1, 1][h:]), 0, 1)
    e1 = to_dp(plus(b[1, 0], (0, up[:h]), (h, side[:h])), 1, 0)
    e2 = to_dp(plus(b[-1, 0], (h, down[:h]), (h, side[h:])), -1, 0)
    e3 = to_dp(plus(b[0, 1], (0, up[h:]), (0, down[h:])), 0, 1)
    f = lambda a: a.astype(F32)
    return (f(b[0, 0]) + f(e1)) + (f(e2) + f(e3))


def gather_1(g):
    return to_dp(g, 1, 0), to_dp(g, -1, 0), to_dp(g, 0, 1)


def gather_2(got):
    left, right, side = got
    h = left.shape[0] // 2
    return (
        to_dp(cat(side[:h], left[:h]), 1, 0),
        to_dp(cat(side[:h], right[h:]), -1, 0),
        to_dp(cat(left[h:], right[h:]), 0, 1),
    )


def gather_3(got):
    left, right, side = got
    h = left.shape[0] // 2
    q = h // 2
    return to_dp(left[:q], 1, 0), to_dp(right[q:h], -1, 0), to_dp(right[h:], 0, 1)


def gathered(g, s1, s2, s3):
    (left, right, side), (am_t0, ap_t1, bm_bp), (u0, u1, v) = s1, s2, s3
    h = g.shape[0] // 2
    return [
        g, side, left, am_t0[:h], bm_bp[:h], right, ap_t1[:h], bm_bp[h:],
        am_t0[h:], ap_t1[h:], u0, u1, v,
    ]


def tie(*xs):
    return lax.optimization_barrier(xs)


def on_device(base, w_in, w_out, basis, cotangent):
    dp = lax.axis_size("dp")
    sections = lax.axis_size("section")
    last = (lax.axis_index("section") == sections - 1).astype(jnp.int32).reshape(1)
    d = lax.axis_index("dp")
    place = jnp.stack(
        [((d // 2 + dx) % X_SIZE) * 2 + (d % 2 + dy) % 2 for dx, dy in RELATIVE]
    ).astype(jnp.int32)
    micro, tokens, width = base.shape
    rows = tokens // dp
    own = micro * rows
    rank = basis.shape[1]
    w_in, w_out = w_in[0], w_out[0]
    hid = w_in.shape[1]
    tok = jax.ShapeDtypeStruct((own, rank), F32)

    gram = lax.psum(
        lax.dot_general(basis, basis, (((0,), (0,)), ((), ())), precision=HIGHEST), "dp"
    )
    proj = reduce_blocks(project(place, basis, w_in, w_out)).astype(BF)
    base_pre = reduce_blocks(product(place, base, w_in, dp))
    p1 = gather_1(proj)
    p2 = gather_2(p1)
    p3 = gather_3(p2)
    up, down = assemble(place, gathered(proj, p1, p2, p3), rank, hid)

    base_half = base_pre.astype(BF)
    s1 = gather_1(base_half)
    part = call(first_kernel, tok, base_pre, down)
    got = hop(part, 1)
    part = call(forward_kernel, tok, base_pre, up, down, gram, *got)
    got = hop(part, 1)
    got, s1 = tie(got, s1)
    s2 = gather_2(s1)
    part = call(forward_kernel, tok, base_pre, up, down, gram, *got)
    got = hop(part, 1)
    c_in, coef_part, slope = call(
        middle_kernel,
        (jax.ShapeDtypeStruct((own, rank), BF), tok, jax.ShapeDtypeStruct((own, hid), F32)),
        base_pre, up, down, gram, *got,
    )

    def back(got):
        return call(backward_kernel, (tok, tok), last_ref, slope, up, down, gram, cot, *got)

    last_ref = last
    cot = cotangent.reshape(own, rank)
    c_pair = cat(c_in, to_dp(c_in, 0, 1))
    _, part = back((cot, cot))
    got = hop(part, -1)
    got, s2, c_pair = tie(got, s2, c_pair)
    s3 = gather_3(s2)
    c_far = [to_dp(c_pair, dx, 0) for dx in (1, -1, 2)]
    _, part = back(got)
    got = hop(part, -1)
    got, s3, c_far = tie(got, s3, c_far)
    xt, hidden_all, slope_all = prepare(
        place, base, dp, basis, [c_pair, *c_far], up, gathered(base_half, s1, s2, s3)
    )
    _, part = back(got)
    got = hop(part, -1)
    g_out, grad_part = back(got)
    g_all = lax.all_to_all(jnp.broadcast_to(g_out[None], (dp, own, rank)), "dp", 0, 0, tiled=True)
    grad_up, down_coefs = finish(place, g_all, down, xt, hidden_all, slope_all)
    parts = cat(coef_part, grad_part)
    parts = parts + to_tensor(parts, 1)
    parts = (parts + to_tensor(parts, 2)).reshape(2, 1, micro, rows, rank)
    return parts[0], parts[1], grad_up[None], down_coefs[None]


def solution(mesh):
    return jax.shard_map(
        on_device,
        mesh=mesh,
        in_specs=(
            P(None, None, "dp"),
            P("section", "dp", "tensor"),
            P("section", "tensor", "dp"),
            P("dp", None),
            P(None, "dp", None),
        ),
        out_specs=(
            P("section", None, "dp", None),
            P("section", None, "dp", None),
            P("section", "dp", "tensor"),
            P("section", "tensor", None),
        ),
        check_vma=False,
    )
```

```python
import functools

import jax
import jax.numpy as jnp
from jax import lax
from jax.experimental import pallas as pl
from jax.experimental.pallas import tpu as pltpu
from jax.sharding import PartitionSpec as P

BF = jnp.bfloat16
F32 = jnp.float32
HIGHEST = lax.Precision.HIGHEST
NT = (((1,), (1,)), ((), ()))
CHUNK = 512
X_SIZE = 4
RELATIVE = ((0, 0), (0, 1), (-1, 0), (-1, 1), (1, 0), (1, 1), (2, 0), (2, 1))
EARLY, LATE = (7, 6, 3, 5), (2, 4, 1, 0)
PARAMS = pltpu.CompilerParams(vmem_limit_bytes=48 * 1024 * 1024)
SMALL = pltpu.CompilerParams(vmem_limit_bytes=16 * 1024 * 1024)


def split2(x):
    hi = x.astype(BF)
    return hi, (x - hi.astype(F32)).astype(BF)


def mm(a, b):
    return jnp.dot(a, b, preferred_element_type=F32)


def mm_nt(a, b):
    return lax.dot_general(a, b, NT, preferred_element_type=F32)


def sigma(v):
    return 0.5 * jnp.tanh(0.5 * v) + 0.5


def wide(x):
    return jnp.concatenate(split2(x), axis=1)


def tall(x):
    return jnp.concatenate(split2(x), axis=0)


def twice(x):
    return jnp.concatenate([x, x], axis=0)


def chunks_of(width):
    return [slice(i, i + CHUNK) for i in range(0, width, CHUNK)]


def gram_share(x, gram):
    return 0.25 * jnp.dot(x, gram, precision=HIGHEST, preferred_element_type=F32)


def first_kernel(base_ref, down_ref, part_ref):
    acc = jnp.zeros(part_ref.shape, F32)
    for cols in chunks_of(base_ref.shape[1]):
        pre = base_ref[:, cols]
        hidden = (pre * sigma(pre)).astype(BF)
        acc += mm_nt(hidden, down_ref[:, cols])
    part_ref[...] = acc


def forward_kernel(base_ref, up_ref, down_ref, gram_ref, r0, r1, part_ref):
    c = r0[...] + r1[...]
    cw = wide(c)
    acc = gram_share(c, gram_ref[...])
    for cols in chunks_of(base_ref.shape[1]):
        pre = base_ref[:, cols] + mm(cw, twice(up_ref[:, cols]))
        hidden = (pre * sigma(pre)).astype(BF)
        acc += mm_nt(hidden, down_ref[:, cols])
    part_ref[...] = acc


def middle_kernel(base_ref, up_ref, down_ref, gram_ref, r0, r1, c_ref, part_ref, slope_ref):
    c = r0[...] + r1[...]
    c_ref[...] = c.astype(BF)
    cw = wide(c)
    acc = gram_share(c, gram_ref[...])
    for cols in chunks_of(base_ref.shape[1]):
        pre = base_ref[:, cols] + mm(cw, twice(up_ref[:, cols]))
        sig = sigma(pre)
        hidden = (pre * sig).astype(BF)
        slope_ref[:, cols] = sig * (1.0 + pre * (1.0 - sig))
        acc += mm_nt(hidden, down_ref[:, cols])
    part_ref[...] = acc


def backward_kernel(last_ref, slope_ref, up_ref, down_ref, gram_ref, cot_ref, r0, r1, g_ref, part_ref):
    g = jnp.where(last_ref[0] == 1, cot_ref[...], r0[...] + r1[...])
    g_ref[...] = g
    gw = wide(g)
    acc = gram_share(g, gram_ref[...])
    for cols in chunks_of(slope_ref.shape[1]):
        g_pre = mm(gw, twice(down_ref[:, cols])) * slope_ref[:, cols]
        hi, lo = split2(g_pre)
        acc += mm_nt(hi, up_ref[:, cols]) + mm_nt(lo, up_ref[:, cols])
    part_ref[...] = acc


def call(kernel, outs, *args):
    return pl.pallas_call(kernel, out_shape=outs, compiler_params=SMALL)(*args)


def base_specs(base, dp, blocks):
    micro, tokens, width = base.shape
    return [
        pl.BlockSpec((micro, tokens // dp, width), lambda i, p, j=j: (0, p[j], 0)) for j in blocks
    ]


def product_kernel(count, with_basis, place_ref, *refs):
    bases, w_ref, refs = refs[:count], refs[count], refs[count + 1 :]
    own = bases[0].shape[0] * bases[0].shape[1]
    if with_basis:
        basis_ref, w_out_ref, refs = refs[0], refs[1], refs[2:]
        rank = basis_ref.shape[1]
    outs, rows = refs[:-1], refs[-1]

    @pl.when(pl.program_id(0) == 0)
    def _():
        for j, b in enumerate(bases):
            rows[j * own : (j + 1) * own] = b[...].reshape(own, b.shape[2])
        if with_basis:
            rows[count * own :] = tall(basis_ref[...].T)

    res = mm(rows[...], w_ref[...])
    for j in range(count):
        outs[j][...] = res[j * own : (j + 1) * own].astype(BF)
    if with_basis:
        up, both = outs[count:]
        up[...] = (res[count * own : count * own + rank] + res[count * own + rank :]).astype(BF)
        down = mm(w_out_ref[...], wide(basis_ref[...]))
        both[...] = (down[:, :rank] + down[:, rank:]).T.astype(BF)


def product(place, base, w_in, dp, blocks, basis=None, w_out=None):
    micro, tokens, width = base.shape
    hid = w_in.shape[1]
    own = micro * tokens // dp
    count = len(blocks)
    column = lambda rows: pl.BlockSpec((rows, CHUNK), lambda i, p: (0, i))
    in_specs = base_specs(base, dp, blocks) + [column(width)]
    shapes, height, more = [own] * count, own * count, ()
    if basis is not None:
        rank = basis.shape[1]
        in_specs += [
            pl.BlockSpec(basis.shape, lambda i, p: (0, 0)),
            pl.BlockSpec((CHUNK, width), lambda i, p: (i, 0)),
        ]
        shapes, height, more = shapes + [rank, rank], height + 2 * rank, (basis, w_out)
    return pl.pallas_call(
        functools.partial(product_kernel, count, basis is not None),
        out_shape=[jax.ShapeDtypeStruct((rows, hid), BF) for rows in shapes],
        grid_spec=pltpu.PrefetchScalarGridSpec(
            num_scalar_prefetch=1,
            grid=(hid // CHUNK,),
            in_specs=in_specs,
            out_specs=[column(rows) for rows in shapes],
            scratch_shapes=[pltpu.VMEM((height, width), BF)],
        ),
        compiler_params=PARAMS,
    )(place, *([base] * count), w_in, *more)


def assemble_kernel(steps, place_ref, *refs):
    pieces, (up_ref, down_ref, gram_ref) = refs[:-3], refs[-3:]
    rows = up_ref.shape[1]
    step = pl.program_id(0)
    flat = jnp.concatenate([p[...] for p in pieces], axis=0)

    @pl.when(step < steps)
    def _():
        for j in range(len(RELATIVE)):
            up_ref[place_ref[j]] = flat[2 * j * rows : (2 * j + 1) * rows]
            down_ref[place_ref[j]] = flat[(2 * j + 1) * rows : (2 * j + 2) * rows]

    @pl.when(step >= steps)
    def _():
        total = flat[: 2 * rows].astype(F32)
        for j in range(1, len(RELATIVE)):
            total += flat[2 * j * rows : (2 * j + 2) * rows].astype(F32)
        gram_ref[...] = jnp.where(step == steps, total, gram_ref[...] + total)


def assemble(place, pieces, rank, hid):
    count = len(RELATIVE)
    steps = hid // CHUNK
    rows = rank // count
    shape = (count, rows, hid)
    spec = pl.BlockSpec((count, rows, CHUNK), lambda i, p: (0, 0, jnp.minimum(i, steps - 1)))
    up, down, gram = pl.pallas_call(
        functools.partial(assemble_kernel, steps),
        out_shape=[jax.ShapeDtypeStruct(shape, BF)] * 2
        + [jax.ShapeDtypeStruct((2 * rows, CHUNK), F32)],
        grid_spec=pltpu.PrefetchScalarGridSpec(
            num_scalar_prefetch=1,
            grid=(pieces[0][0].shape[1] // CHUNK,),
            in_specs=piece_specs(pieces),
            out_specs=[spec, spec, pl.BlockSpec((2 * rows, CHUNK), lambda i, p: (0, 0))],
        ),
        compiler_params=SMALL,
    )(place, *[a for a, _, _ in pieces])
    return up.reshape(rank, hid), down.reshape(rank, hid), gram.reshape(rank, rank)


def copy_kernel(plan, count, *refs):
    for out, parts in zip(refs[count:], plan):
        out[...] = jnp.concatenate([refs[k][a:b] for k, a, b in parts], axis=0)


def copies(arrays, plan):
    hid = arrays[0].shape[1]
    heights = [sum(b - a for _, a, b in parts) for parts in plan]
    column = lambda rows: pl.BlockSpec((rows, CHUNK), lambda i: (0, i))
    return pl.pallas_call(
        functools.partial(copy_kernel, plan, len(arrays)),
        out_shape=[jax.ShapeDtypeStruct((rows, hid), BF) for rows in heights],
        grid=(hid // CHUNK,),
        in_specs=[column(a.shape[0]) for a in arrays],
        out_specs=[column(rows) for rows in heights],
        compiler_params=SMALL,
    )(*arrays)


def prepare_kernel(count, place_ref, *refs):
    bases, refs = refs[:count], refs[count:]
    half = count // 2
    basis_ref, c_refs, up_ref, pieces = refs[0], refs[1 : 1 + half], refs[1 + half], refs[2 + half : -3]
    xt_ref, hidden_ref, slope_ref = refs[-3:]
    own = bases[0].shape[0] * bases[0].shape[1]

    @pl.when(pl.program_id(0) == 0)
    def _():
        basis = basis_ref[...].astype(BF)
        for j, b in enumerate(bases):
            c = c_refs[j // 2][(j % 2) * own : (j % 2 + 1) * own]
            x = b[...].reshape(own, b.shape[2]).astype(F32) + mm_nt(c, basis)
            xt_ref[:, j * own : (j + 1) * own] = x.T.astype(BF)

    up = up_ref[...]
    start = 0
    c_all = jnp.concatenate([c[...] for c in c_refs], axis=0)
    for p in pieces:
        rows = slice(start, start + p.shape[0])
        start += p.shape[0]
        pre = p[...].astype(F32) + mm(c_all[rows], up)
        sig = sigma(pre)
        hidden = pre * sig
        hidden_ref[rows] = hidden.astype(BF)
        slope_ref[rows] = (sig + hidden * (1.0 - sig)).astype(BF)


def prepare(place, base, dp, blocks, basis, c_pieces, up, pieces):
    micro, tokens, width = base.shape
    hid = up.shape[1]
    every = micro * tokens // dp * len(blocks)
    whole = lambda a: pl.BlockSpec(a.shape, lambda i, p: (0, 0))
    column = lambda rows: pl.BlockSpec((rows, CHUNK), lambda i, p: (0, i))
    return pl.pallas_call(
        functools.partial(prepare_kernel, len(blocks)),
        out_shape=[
            jax.ShapeDtypeStruct((width, every), BF),
            jax.ShapeDtypeStruct((every, hid), BF),
            jax.ShapeDtypeStruct((every, hid), BF),
        ],
        grid_spec=pltpu.PrefetchScalarGridSpec(
            num_scalar_prefetch=1,
            grid=(hid // CHUNK,),
            in_specs=base_specs(base, dp, blocks)
            + [whole(basis)]
            + [whole(c) for c in c_pieces]
            + [column(up.shape[0])]
            + piece_specs(pieces),
            out_specs=[
                pl.BlockSpec((width, every), lambda i, p: (0, 0)),
                column(every),
                column(every),
            ],
        ),
        compiler_params=PARAMS,
    )(place, *([base] * len(blocks)), basis, *c_pieces, up, *[a for a, _, _ in pieces])


def finish_kernel(place_ref, g_ref, down_ref, xt0, hidden0, slope0, xt1, hidden1, slope1, *refs):
    grad_ref, dc_ref, gw, gt = refs
    rank = down_ref.shape[0]
    own = g_ref.shape[1]

    @pl.when(pl.program_id(0) == 0)
    def _():
        for j in range(len(RELATIVE)):
            g = g_ref[place_ref[j]]
            gw[j * own : (j + 1) * own] = wide(g)
            gt[:, j * own : (j + 1) * own] = tall(g.T)

    h = gw.shape[0] // 2
    down2 = twice(down_ref[...])
    low = (mm(gw[:h], down2) * slope0[...].astype(F32)).astype(BF)
    high = (mm(gw[h:], down2) * slope1[...].astype(F32)).astype(BF)
    grad_ref[...] = (mm(xt0[...], low) + mm(xt1[...], high)).astype(BF)
    dc = mm(gt[:, :h], hidden0[...]) + mm(gt[:, h:], hidden1[...])
    dc_ref[...] = (dc[:rank] + dc[rank:]).T


def finish(place, g_all, down, first, second):
    rank, hid = down.shape
    width, every = first[0].shape
    column = lambda rows: pl.BlockSpec((rows, CHUNK), lambda i, p: (0, i))
    part = [pl.BlockSpec((width, every), lambda i, p: (0, 0)), column(every), column(every)]
    return pl.pallas_call(
        finish_kernel,
        out_shape=[jax.ShapeDtypeStruct((width, hid), BF), jax.ShapeDtypeStruct((hid, rank), F32)],
        grid_spec=pltpu.PrefetchScalarGridSpec(
            num_scalar_prefetch=1,
            grid=(hid // CHUNK,),
            in_specs=[pl.BlockSpec(g_all.shape, lambda i, p: (0, 0, 0)), column(rank)] + part + part,
            out_specs=[column(width), pl.BlockSpec((CHUNK, rank), lambda i, p: (i, 0))],
            scratch_shapes=[
                pltpu.VMEM((2 * every, 2 * rank), BF),
                pltpu.VMEM((2 * rank, 2 * every), BF),
            ],
        ),
        compiler_params=PARAMS,
    )(place, g_all, down, *first, *second)


def to_dp(x, dx, dy):
    size = lax.axis_size("dp")
    pairs = [(i, ((i // 2 + dx) % X_SIZE) * 2 + ((i % 2) ^ dy)) for i in range(size)]
    return lax.ppermute(x, "dp", pairs)


def to_tensor(x, k):
    size = lax.axis_size("tensor")
    return lax.ppermute(x, "tensor", [(t, t ^ k) for t in range(size)])


def hop(part, by, *beside):
    sections, tensors = lax.axis_size("section"), lax.axis_size("tensor")
    pair_sum = part + to_tensor(part, 1)
    pair_sum, *beside = tie(pair_sum, *beside)
    pairs = [
        (s * tensors + t, (s + by) * tensors + (t ^ (2 * (t % 2))))
        for s in range(sections)
        for t in range(tensors)
        if 0 <= s + by < sections
    ]
    got = lax.ppermute(pair_sum, ("section", "tensor"), pairs)
    return (got, to_tensor(got, 1), *beside)


def cat(*xs):
    return jnp.concatenate(xs, axis=0)


def plus(x, *ys):
    total = x.astype(F32)
    for start, y in ys:
        pads = ((start, x.shape[0] - start - y.shape[0]), (0, 0))
        total = total + jnp.pad(y.astype(F32), pads)
    return total.astype(x.dtype)


def reduce_blocks(blocks):
    b = dict(zip(RELATIVE, blocks))
    n = blocks[0].shape[0]
    h, q = n // 2, n // 4
    far = b[2, 1]
    u0, u1, v = to_dp(far[:q], 1, 0), to_dp(far[q:h], -1, 0), to_dp(far[h:], 0, 1)
    up = to_dp(cat(b[2, 0][:h], plus(b[1, 1][:h], (0, u0))), 1, 0)
    down = to_dp(cat(plus(b[2, 0][h:], (0, v)), plus(b[-1, 1][:h], (q, u1))), -1, 0)
    side = to_dp(cat(b[1, 1][h:], b[-1, 1][h:]), 0, 1)
    e1 = to_dp(plus(b[1, 0], (0, up[:h]), (h, side[:h])), 1, 0)
    e2 = to_dp(plus(b[-1, 0], (h, down[:h]), (h, side[h:])), -1, 0)
    e3 = to_dp(plus(b[0, 1], (0, up[h:]), (0, down[h:])), 0, 1)
    f = lambda a: a.astype(F32)
    return (f(b[0, 0]) + f(e1)) + (f(e2) + f(e3))


def gather_1(g):
    return to_dp(g, 1, 0), to_dp(g, -1, 0), to_dp(g, 0, 1)


def gather_2(got):
    n = got[0].shape[0]
    h = n // 2
    left, right, side = copies(
        got, [[(2, 0, h), (0, 0, h)], [(2, 0, h), (1, h, n)], [(0, h, n), (1, h, n)]]
    )
    return to_dp(left, 1, 0), to_dp(right, -1, 0), to_dp(side, 0, 1)


def gather_3(got):
    h = got[0].shape[0] // 2
    q = h // 2
    left, right, side = copies(got, [[(0, 0, q)], [(1, q, h)], [(1, h, 2 * h)]])
    return to_dp(left, 1, 0), to_dp(right, -1, 0), to_dp(side, 0, 1)


def gathered(g, s1, s2, s3):
    (left, right, side), (am_t0, ap_t1, bm_bp), (u0, u1, v) = s1, s2, s3
    whole = lambda a: (a, 0, a.shape[0])
    low = lambda a: (a, 0, a.shape[0] // 2)
    high = lambda a: (a, 1, a.shape[0] // 2)
    return (
        [whole(g), whole(side), whole(left), low(am_t0), low(bm_bp)],
        [
            whole(right), low(ap_t1), high(bm_bp), high(am_t0), high(ap_t1),
            whole(u0), whole(u1), whole(v),
        ],
    )


def piece_specs(pieces):
    return [pl.BlockSpec((n, CHUNK), lambda i, p, k=k: (k, i)) for _, k, n in pieces]


def tie(*xs):
    return lax.optimization_barrier(xs)


def on_device(base, w_in, w_out, basis, cotangent):
    dp = lax.axis_size("dp")
    sections = lax.axis_size("section")
    last = (lax.axis_index("section") == sections - 1).astype(jnp.int32).reshape(1)
    d = lax.axis_index("dp")
    place = jnp.stack(
        [((d // 2 + dx) % X_SIZE) * 2 + (d % 2 + dy) % 2 for dx, dy in RELATIVE]
    ).astype(jnp.int32)
    micro, tokens, width = base.shape
    rows = tokens // dp
    own = micro * rows
    rank = basis.shape[1]
    w_in, w_out = w_in[0], w_out[0]
    hid = w_in.shape[1]
    tok = jax.ShapeDtypeStruct((own, rank), F32)

    blocks = [None] * len(RELATIVE)
    *early, up_part, down_part = product(place, base, w_in, dp, EARLY, basis, w_out)
    for j, block in zip(EARLY, early):
        blocks[j] = block
    for j, block in zip(LATE, product(place, base, w_in, dp, LATE)):
        blocks[j] = block
    share = rank // dp
    proj = reduce_blocks(
        [
            cat(*(lax.dynamic_slice_in_dim(x, place[j] * share, share) for x in (up_part, down_part)))
            for j in range(len(RELATIVE))
        ]
    ).astype(BF)
    gram_part = lax.dot_general(basis, basis, (((0,), (0,)), ((), ())), precision=HIGHEST)
    gram_part = split2(gram_part.reshape(2 * share, -1))
    proj = jnp.concatenate([proj, *gram_part], axis=1)
    base_pre = reduce_blocks(blocks)
    p1 = gather_1(proj)
    p2 = gather_2(p1)
    p3 = gather_3(p2)
    up, down, gram = assemble(place, sum(gathered(proj, p1, p2, p3), []), rank, hid)

    base_half = base_pre.astype(BF)
    s1 = gather_1(base_half)
    part = call(first_kernel, tok, base_pre, down)
    got = hop(part, 1)
    part = call(forward_kernel, tok, base_pre, up, down, gram, *got)
    got = hop(part, 1)
    part = call(forward_kernel, tok, base_pre, up, down, gram, *got)
    *got, s1 = hop(part, 1, s1)
    s2 = gather_2(s1)
    c_in, coef_part, slope = call(
        middle_kernel,
        (jax.ShapeDtypeStruct((own, rank), BF), tok, jax.ShapeDtypeStruct((own, hid), F32)),
        base_pre, up, down, gram, *got,
    )
    cot = cotangent.reshape(own, rank)

    def back(got):
        return call(backward_kernel, (tok, tok), last, slope, up, down, gram, cot, *got)

    c_pair = cat(c_in, to_dp(c_in, 0, 1))
    _, part = back((cot, cot))
    got = hop(part, -1)
    _, part = back(got)
    *got, s2, c_pair = hop(part, -1, s2, c_pair)
    s3 = gather_3(s2)
    c_far = [to_dp(c_pair, dx, 0) for dx in (-1, 1, 2)]
    _, part = back(got)
    *got, s2, s3, c_far = hop(part, -1, s2, s3, c_far)
    left, right, far = c_far[1], c_far[0], c_far[2]
    pieces = gathered(base_half, s1, s2, s3)
    first = prepare(place, base, dp, range(4), basis, [c_pair, left], up, pieces[0])
    *got, first = tie(*got, first)
    second = prepare(place, base, dp, range(4, 8), basis, [right, far], up, pieces[1])
    g_out = jnp.where(last[0] == 1, cot, got[0] + got[1])
    g_all = lax.all_to_all(jnp.broadcast_to(g_out[None], (dp, own, rank)), "dp", 0, 0, tiled=True)
    _, grad_part = back(got)
    grad_up, down_coefs = finish(place, g_all, down, first, second)
    parts = cat(coef_part, grad_part)
    parts = parts + to_tensor(parts, 1)
    parts = (parts + to_tensor(parts, 2)).reshape(2, 1, micro, rows, rank)
    return parts[0], parts[1], grad_up[None], down_coefs[None]


def solution(mesh):
    return jax.shard_map(
        on_device,
        mesh=mesh,
        in_specs=(
            P(None, None, "dp"),
            P("section", "dp", "tensor"),
            P("section", "tensor", "dp"),
            P("dp", None),
            P(None, "dp", None),
        ),
        out_specs=(
            P("section", None, "dp", None),
            P("section", None, "dp", None),
            P("section", "dp", "tensor"),
            P("section", "tensor", None),
        ),
        check_vma=False,
    )
```

```python
import functools

import jax
import jax.numpy as jnp
from jax import lax
from jax.experimental import pallas as pl
from jax.experimental.pallas import tpu as pltpu
from jax.sharding import PartitionSpec as P

BF = jnp.bfloat16
F32 = jnp.float32
HIGHEST = lax.Precision.HIGHEST
NT = (((1,), (1,)), ((), ()))
CHUNK = 512
X_SIZE = 4
RELATIVE = ((0, 0), (0, 1), (-1, 0), (-1, 1), (1, 0), (1, 1), (2, 0), (2, 1))
EARLY, LATE = (7, 6, 3, 5), (2, 4, 1, 0)
PARAMS = pltpu.CompilerParams(vmem_limit_bytes=48 * 1024 * 1024)
SMALL = pltpu.CompilerParams(vmem_limit_bytes=16 * 1024 * 1024)


def split2(x):
    hi = x.astype(BF)
    return hi, (x - hi.astype(F32)).astype(BF)


def mm(a, b):
    return jnp.dot(a, b, preferred_element_type=F32)


def mm_nt(a, b):
    return lax.dot_general(a, b, NT, preferred_element_type=F32)


def sigma(v):
    return 0.5 * jnp.tanh(0.5 * v) + 0.5


def wide(x):
    return jnp.concatenate(split2(x), axis=1)


def tall(x):
    return jnp.concatenate(split2(x), axis=0)


def twice(x):
    return jnp.concatenate([x, x], axis=0)


def chunks_of(width):
    return [slice(i, i + CHUNK) for i in range(0, width, CHUNK)]


def gram_share(x, gram):
    return 0.25 * jnp.dot(x, gram, precision=HIGHEST, preferred_element_type=F32)


def first_kernel(base_ref, down_ref, part_ref):
    acc = jnp.zeros(part_ref.shape, F32)
    for cols in chunks_of(base_ref.shape[1]):
        pre = base_ref[:, cols].astype(F32)
        hidden = (pre * sigma(pre)).astype(BF)
        acc += mm_nt(hidden, down_ref[:, cols])
    part_ref[...] = acc


def forward_kernel(base_ref, up_ref, down_ref, gram_ref, r0, r1, part_ref):
    c = r0[...] + r1[...]
    cw = wide(c)
    acc = gram_share(c, gram_ref[...])
    for cols in chunks_of(base_ref.shape[1]):
        pre = base_ref[:, cols].astype(F32) + mm(cw, twice(up_ref[:, cols]))
        hidden = (pre * sigma(pre)).astype(BF)
        acc += mm_nt(hidden, down_ref[:, cols])
    part_ref[...] = acc


def middle_kernel(base_ref, up_ref, down_ref, gram_ref, r0, r1, c_ref, part_ref, slope_ref):
    c = r0[...] + r1[...]
    c_ref[...] = c.astype(BF)
    cw = wide(c)
    acc = gram_share(c, gram_ref[...])
    for cols in chunks_of(base_ref.shape[1]):
        pre = base_ref[:, cols].astype(F32) + mm(cw, twice(up_ref[:, cols]))
        sig = sigma(pre)
        hidden = (pre * sig).astype(BF)
        slope_ref[:, cols] = (sig * (1.0 + pre * (1.0 - sig))).astype(BF)
        acc += mm_nt(hidden, down_ref[:, cols])
    part_ref[...] = acc


def backward_kernel(last_ref, slope_ref, up_ref, down_ref, gram_ref, cot_ref, r0, r1, g_ref, part_ref):
    g = jnp.where(last_ref[0] == 1, cot_ref[...], r0[...] + r1[...])
    g_ref[...] = g
    gw = wide(g)
    acc = gram_share(g, gram_ref[...])
    for cols in chunks_of(slope_ref.shape[1]):
        g_pre = mm(gw, twice(down_ref[:, cols])) * slope_ref[:, cols].astype(F32)
        hi, lo = split2(g_pre)
        acc += mm_nt(hi, up_ref[:, cols]) + mm_nt(lo, up_ref[:, cols])
    part_ref[...] = acc


def call(kernel, outs, *args):
    return pl.pallas_call(kernel, out_shape=outs, compiler_params=SMALL)(*args)


def base_specs(base, dp, blocks):
    micro, tokens, width = base.shape
    return [
        pl.BlockSpec((micro, tokens // dp, width), lambda i, p, j=j: (0, p[j], 0)) for j in blocks
    ]


def product_kernel(count, place_ref, *refs):
    bases, w_ref, outs, rows = refs[:count], refs[count], refs[count + 1 : -1], refs[-1]
    own = bases[0].shape[0] * bases[0].shape[1]

    @pl.when(pl.program_id(0) == 0)
    def _():
        for j, b in enumerate(bases):
            rows[j * own : (j + 1) * own] = b[...].reshape(own, b.shape[2])

    res = mm(rows[...], w_ref[...])
    for j, out in enumerate(outs):
        out[...] = res[j * own : (j + 1) * own].astype(BF)


def product(place, base, w_in, dp, blocks):
    micro, tokens, width = base.shape
    hid = w_in.shape[1]
    own = micro * tokens // dp
    count = len(blocks)
    column = lambda rows: pl.BlockSpec((rows, CHUNK), lambda i, p: (0, i))
    return pl.pallas_call(
        functools.partial(product_kernel, count),
        out_shape=[jax.ShapeDtypeStruct((own, hid), BF)] * count,
        grid_spec=pltpu.PrefetchScalarGridSpec(
            num_scalar_prefetch=1,
            grid=(hid // CHUNK,),
            in_specs=base_specs(base, dp, blocks) + [column(width)],
            out_specs=[column(own)] * count,
            scratch_shapes=[pltpu.VMEM((own * count, width), BF)],
        ),
        compiler_params=PARAMS,
    )(place, *([base] * count), w_in)


def project_kernel(basis_ref, w_in_ref, w_out_ref, out_ref, wide_ref, tall_ref):
    rank = basis_ref.shape[1]
    count, rows, cols = out_ref.shape
    share = rows // 2

    @pl.when(pl.program_id(0) == 0)
    def _():
        wide_ref[...] = wide(basis_ref[...])
        tall_ref[...] = tall(basis_ref[...].T)

    up = mm(tall_ref[...], w_in_ref[...])
    down = mm(w_out_ref[...], wide_ref[...])
    out_ref[:, :share] = (up[:rank] + up[rank:]).astype(BF).reshape(count, share, cols)
    down = (down[:, :rank] + down[:, rank:]).T
    out_ref[:, share:] = down.astype(BF).reshape(count, share, cols)


def project(basis, w_in, w_out, dp):
    width, rank = basis.shape
    hid = w_in.shape[1]
    rows = 2 * rank // dp
    return pl.pallas_call(
        project_kernel,
        out_shape=jax.ShapeDtypeStruct((dp, rows, hid), BF),
        grid=(hid // CHUNK,),
        in_specs=[
            pl.BlockSpec((width, rank), lambda i: (0, 0)),
            pl.BlockSpec((width, CHUNK), lambda i: (0, i)),
            pl.BlockSpec((CHUNK, width), lambda i: (i, 0)),
        ],
        out_specs=pl.BlockSpec((dp, rows, CHUNK), lambda i: (0, 0, i)),
        scratch_shapes=[pltpu.VMEM((width, 2 * rank), BF), pltpu.VMEM((2 * rank, width), BF)],
        compiler_params=PARAMS,
    )(basis, w_in, w_out)


def assemble_kernel(steps, all_ref, up_ref, down_ref, gram_ref):
    share = up_ref.shape[1]
    step = pl.program_id(0)

    @pl.when(step < steps)
    def _():
        up_ref[...] = all_ref[:, :share]
        down_ref[...] = all_ref[:, share:]

    @pl.when(step >= steps)
    def _():
        total = jnp.sum(all_ref[...].astype(F32), axis=0)
        gram_ref[...] = jnp.where(step == steps, total, gram_ref[...] + total)


def assemble(everyone, hid):
    count, rows, cols = everyone.shape
    steps = hid // CHUNK
    share = rows // 2
    rank = count * share
    spec = pl.BlockSpec((count, share, CHUNK), lambda i: (0, 0, jnp.minimum(i, steps - 1)))
    up, down, gram = pl.pallas_call(
        functools.partial(assemble_kernel, steps),
        out_shape=[jax.ShapeDtypeStruct((count, share, hid), BF)] * 2
        + [jax.ShapeDtypeStruct((rows, CHUNK), F32)],
        grid=(cols // CHUNK,),
        in_specs=[pl.BlockSpec((count, rows, CHUNK), lambda i: (0, 0, i))],
        out_specs=[spec, spec, pl.BlockSpec((rows, CHUNK), lambda i: (0, 0))],
        compiler_params=SMALL,
    )(everyone)
    return up.reshape(rank, hid), down.reshape(rank, hid), gram.reshape(rank, rank)


def copy_kernel(plan, count, *refs):
    for out, parts in zip(refs[count:], plan):
        out[...] = jnp.concatenate([refs[k][a:b] for k, a, b in parts], axis=0)


def copies(arrays, plan):
    hid = arrays[0].shape[1]
    heights = [sum(b - a for _, a, b in parts) for parts in plan]
    column = lambda rows: pl.BlockSpec((rows, CHUNK), lambda i: (0, i))
    return pl.pallas_call(
        functools.partial(copy_kernel, plan, len(arrays)),
        out_shape=[jax.ShapeDtypeStruct((rows, hid), BF) for rows in heights],
        grid=(hid // CHUNK,),
        in_specs=[column(a.shape[0]) for a in arrays],
        out_specs=[column(rows) for rows in heights],
        compiler_params=SMALL,
    )(*arrays)


def prepare_kernel(count, place_ref, *refs):
    bases, refs = refs[:count], refs[count:]
    half = count // 2
    basis_ref, c_refs, up_ref, pieces = refs[0], refs[1 : 1 + half], refs[1 + half], refs[2 + half : -3]
    xt_ref, hidden_ref, slope_ref = refs[-3:]
    own = bases[0].shape[0] * bases[0].shape[1]

    @pl.when(pl.program_id(0) == 0)
    def _():
        basis = basis_ref[...].astype(BF)
        for j, b in enumerate(bases):
            c = c_refs[j // 2][(j % 2) * own : (j % 2 + 1) * own]
            x = b[...].reshape(own, b.shape[2]).astype(F32) + mm_nt(c, basis)
            xt_ref[:, j * own : (j + 1) * own] = x.T.astype(BF)

    up = up_ref[...]
    start = 0
    c_all = jnp.concatenate([c[...] for c in c_refs], axis=0)
    for p in pieces:
        rows = slice(start, start + p.shape[0])
        start += p.shape[0]
        pre = p[...].astype(F32) + mm(c_all[rows], up)
        sig = sigma(pre)
        hidden = pre * sig
        hidden_ref[rows] = hidden.astype(BF)
        slope_ref[rows] = (sig + hidden * (1.0 - sig)).astype(BF)


def prepare(place, base, dp, blocks, basis, c_pieces, up, pieces):
    micro, tokens, width = base.shape
    hid = up.shape[1]
    every = micro * tokens // dp * len(blocks)
    whole = lambda a: pl.BlockSpec(a.shape, lambda i, p: (0, 0))
    column = lambda rows: pl.BlockSpec((rows, CHUNK), lambda i, p: (0, i))
    return pl.pallas_call(
        functools.partial(prepare_kernel, len(blocks)),
        out_shape=[
            jax.ShapeDtypeStruct((width, every), BF),
            jax.ShapeDtypeStruct((every, hid), BF),
            jax.ShapeDtypeStruct((every, hid), BF),
        ],
        grid_spec=pltpu.PrefetchScalarGridSpec(
            num_scalar_prefetch=1,
            grid=(hid // CHUNK,),
            in_specs=base_specs(base, dp, blocks)
            + [whole(basis)]
            + [whole(c) for c in c_pieces]
            + [column(up.shape[0])]
            + piece_specs(pieces),
            out_specs=[
                pl.BlockSpec((width, every), lambda i, p: (0, 0)),
                column(every),
                column(every),
            ],
        ),
        compiler_params=PARAMS,
    )(place, *([base] * len(blocks)), basis, *c_pieces, up, *[a for a, _, _ in pieces])


def finish_kernel(groups, place_ref, g_ref, down_ref, *refs):
    grad_ref, dc_ref, gw, gt = refs[-4:]
    rank = down_ref.shape[0]
    own = g_ref.shape[1]

    @pl.when(pl.program_id(0) == 0)
    def _():
        for j in range(len(RELATIVE)):
            g = g_ref[place_ref[j]]
            gw[j * own : (j + 1) * own] = wide(g)
            gt[:, j * own : (j + 1) * own] = tall(g.T)

    down2 = twice(down_ref[...])
    start, grad, dc = 0, 0.0, 0.0
    for k in range(groups):
        xt, hidden, slope = refs[3 * k : 3 * k + 3]
        stop = start + hidden.shape[0]
        g_pre = (mm(gw[start:stop], down2) * slope[...].astype(F32)).astype(BF)
        grad += mm(xt[...], g_pre)
        dc += mm(gt[:, start:stop], hidden[...])
        start = stop
    grad_ref[...] = grad.astype(BF)
    dc_ref[...] = (dc[:rank] + dc[rank:]).T


def finish(place, g_all, down, groups):
    rank, hid = down.shape
    width = groups[0][0].shape[0]
    every = sum(xt.shape[1] for xt, _, _ in groups)
    column = lambda rows: pl.BlockSpec((rows, CHUNK), lambda i, p: (0, i))
    specs = []
    for xt, hidden, slope in groups:
        specs += [pl.BlockSpec(xt.shape, lambda i, p: (0, 0)), column(hidden.shape[0]), column(hidden.shape[0])]
    return pl.pallas_call(
        functools.partial(finish_kernel, len(groups)),
        out_shape=[jax.ShapeDtypeStruct((width, hid), BF), jax.ShapeDtypeStruct((hid, rank), F32)],
        grid_spec=pltpu.PrefetchScalarGridSpec(
            num_scalar_prefetch=1,
            grid=(hid // CHUNK,),
            in_specs=[pl.BlockSpec(g_all.shape, lambda i, p: (0, 0, 0)), column(rank)] + specs,
            out_specs=[column(width), pl.BlockSpec((CHUNK, rank), lambda i, p: (i, 0))],
            scratch_shapes=[pltpu.VMEM((every, 2 * rank), BF), pltpu.VMEM((2 * rank, every), BF)],
        ),
        compiler_params=PARAMS,
    )(place, g_all, down, *sum((list(g) for g in groups), []))


def to_dp(x, dx, dy):
    size = lax.axis_size("dp")
    pairs = [(i, ((i // 2 + dx) % X_SIZE) * 2 + ((i % 2) ^ dy)) for i in range(size)]
    return lax.ppermute(x, "dp", pairs)


def to_tensor(x, k):
    size = lax.axis_size("tensor")
    return lax.ppermute(x, "tensor", [(t, t ^ k) for t in range(size)])


def hop(part, by, before=(), during=lambda: ()):
    sections, tensors = lax.axis_size("section"), lax.axis_size("tensor")
    pair_sum, before = tie(part + to_tensor(part, 1), before)
    pairs = [
        (s * tensors + t, (s + by) * tensors + (t ^ (2 * (t % 2))))
        for s in range(sections)
        for t in range(tensors)
        if 0 <= s + by < sections
    ]
    got = lax.ppermute(pair_sum, ("section", "tensor"), pairs)
    got, made = tie(got, during(*before))
    return (got, to_tensor(got, 1)), before, made


def cat(*xs):
    return jnp.concatenate(xs, axis=0)


def plus(x, *ys):
    total = x.astype(F32)
    for start, y in ys:
        pads = ((start, x.shape[0] - start - y.shape[0]), (0, 0))
        total = total + jnp.pad(y.astype(F32), pads)
    return total.astype(x.dtype)


def reduce_blocks(blocks):
    b = dict(zip(RELATIVE, blocks))
    n = blocks[0].shape[0]
    h, q = n // 2, n // 4
    far = b[2, 1]
    u0, u1, v = to_dp(far[:q], 1, 0), to_dp(far[q:h], -1, 0), to_dp(far[h:], 0, 1)
    up = to_dp(cat(b[2, 0][:h], plus(b[1, 1][:h], (0, u0))), 1, 0)
    down = to_dp(cat(plus(b[2, 0][h:], (0, v)), plus(b[-1, 1][:h], (q, u1))), -1, 0)
    side = to_dp(cat(b[1, 1][h:], b[-1, 1][h:]), 0, 1)
    e1 = to_dp(plus(b[1, 0], (0, up[:h]), (h, side[:h])), 1, 0)
    e2 = to_dp(plus(b[-1, 0], (h, down[:h]), (h, side[h:])), -1, 0)
    e3 = to_dp(plus(b[0, 1], (0, up[h:]), (0, down[h:])), 0, 1)
    f = lambda a: a.astype(F32)
    return (f(b[0, 0]) + f(e1)) + (f(e2) + f(e3))


def swap(x):
    return lax.all_to_all(x, "dp", 0, 0, tiled=True)


def whole(a):
    return a, 0, a.shape[0]


def low_half(a):
    return a, 0, a.shape[0] // 2


def high_half(a):
    return a, 1, a.shape[0] // 2


def piece_specs(pieces):
    return [pl.BlockSpec((n, CHUNK), lambda i, p, k=k: (k, i)) for _, k, n in pieces]


def tie(*xs):
    return lax.optimization_barrier(xs)


def on_device(base, w_in, w_out, basis, cotangent):
    dp = lax.axis_size("dp")
    sections = lax.axis_size("section")
    last = (lax.axis_index("section") == sections - 1).astype(jnp.int32).reshape(1)
    d = lax.axis_index("dp")
    place = jnp.stack(
        [((d // 2 + dx) % X_SIZE) * 2 + (d % 2 + dy) % 2 for dx, dy in RELATIVE]
    ).astype(jnp.int32)
    micro, tokens, width = base.shape
    rows = tokens // dp
    own = micro * rows
    rank = basis.shape[1]
    w_in, w_out = w_in[0], w_out[0]
    hid = w_in.shape[1]
    tok = jax.ShapeDtypeStruct((own, rank), F32)

    share = rank // dp
    proj = swap(project(basis, w_in, w_out, dp))
    proj = jnp.sum(proj.astype(F32), axis=0).astype(BF)
    gram_part = lax.dot_general(basis, basis, (((0,), (0,)), ((), ())), precision=HIGHEST)
    gram_part = split2(gram_part.reshape(2 * share, -1))
    proj = jnp.concatenate([proj, *gram_part], axis=1)
    proj = swap(jnp.broadcast_to(proj[None], (dp,) + proj.shape))
    blocks = [None] * len(RELATIVE)
    for group in (EARLY, LATE):
        for j, block in zip(group, product(place, base, w_in, dp, group)):
            blocks[j] = block
    own_pre = reduce_blocks(blocks).astype(BF)
    up, down, gram = assemble(proj, hid)

    h, q = own // 2, own // 4
    left, right = to_dp(own_pre, 1, 0), to_dp(own_pre, -1, 0)
    part = call(first_kernel, tok, own_pre, down)
    got, _, (low,) = hop(part, 1, (own_pre,), lambda a: copies([a], [[(0, 0, h)]]))
    side_low = to_dp(low, 0, 1)
    part = call(forward_kernel, tok, own_pre, up, down, gram, *got)
    got, _, (high,) = hop(part, 1, (own_pre,), lambda a: copies([a], [[(0, h, own)]]))
    side_high = to_dp(high, 0, 1)
    part = call(forward_kernel, tok, own_pre, up, down, gram, *got)
    got, (left, right, side_low), made = hop(
        part,
        1,
        (left, right, side_low),
        lambda *a: copies(a, [[(0, h, own)], [(2, 0, h), (0, 0, h)], [(2, 0, h), (1, h, own)]]),
    )
    left_high = to_dp(made[0], 0, 1)
    two_left, two_right = to_dp(made[1], 1, 0), to_dp(made[2], -1, 0)
    c_in, coef_part, slope = call(
        middle_kernel,
        (jax.ShapeDtypeStruct((own, rank), BF), tok, jax.ShapeDtypeStruct((own, hid), BF)),
        own_pre, up, down, gram, *got,
    )
    cot = cotangent.reshape(own, rank)

    def back(got):
        return call(backward_kernel, (tok, tok), last, slope, up, down, gram, cot, *got)

    c_side = to_dp(c_in, 0, 1)
    _, part = back((cot, cot))
    got, _, (high,) = hop(part, -1, (right,), lambda a: copies([a], [[(0, h, own)]]))
    (got, c_side) = tie(got, c_side)
    c_pair = cat(c_in, c_side)
    c_right, c_left, c_far = [to_dp(c_pair, dx, 0) for dx in (-1, 1, 2)]
    right_high = to_dp(high, 0, 1)
    _, part = back(got)

    def second(two_left, two_right, side_high, c_pair):
        made = copies(
            [two_left, two_right], [[(1, h, own)], [(0, 0, q)], [(1, q, h)]]
        )
        pieces = [whole(own_pre), whole(side_low), whole(side_high)]
        return made, prepare(place, base, dp, range(2), basis, [c_pair], up, pieces)

    got, (two_left, two_right, side_high, c_pair), (made, zero) = hop(
        part, -1, (two_left, two_right, side_high, c_pair), second
    )
    far_high = to_dp(made[0], 0, 1)
    far_0, far_1 = to_dp(made[1], 1, 0), to_dp(made[2], -1, 0)
    _, part = back(got)

    def third(left_high, right_high, c_left, c_right):
        pieces = [
            whole(left), low_half(two_left), whole(left_high),
            whole(right), low_half(two_right), whole(right_high),
        ]
        return prepare(place, base, dp, range(2, 6), basis, [c_left, c_right], up, pieces)

    got, _, one = hop(part, -1, (left_high, right_high, c_left, c_right), third)
    g_out = jnp.where(last[0] == 1, cot, got[0] + got[1])
    g_all = swap(jnp.broadcast_to(g_out[None], (dp, own, rank)))
    pieces = [high_half(two_left), high_half(two_right), whole(far_0), whole(far_1), whole(far_high)]
    two = prepare(place, base, dp, range(6, 8), basis, [c_far], up, pieces)
    _, grad_part = back(got)
    grad_up, down_coefs = finish(place, g_all, down, [zero, one, two])
    parts = cat(coef_part, grad_part)
    parts = parts + to_tensor(parts, 1)
    parts = (parts + to_tensor(parts, 2)).reshape(2, 1, micro, rows, rank)
    return parts[0], parts[1], grad_up[None], down_coefs[None]


def solution(mesh):
    return jax.shard_map(
        on_device,
        mesh=mesh,
        in_specs=(
            P(None, None, "dp"),
            P("section", "dp", "tensor"),
            P("section", "tensor", "dp"),
            P("dp", None),
            P(None, "dp", None),
        ),
        out_specs=(
            P("section", None, "dp", None),
            P("section", None, "dp", None),
            P("section", "dp", "tensor"),
            P("section", "tensor", None),
        ),
        check_vma=False,
    )
```

```python
import functools

import jax
import jax.numpy as jnp
from jax import lax
from jax.experimental import pallas as pl
from jax.experimental.pallas import tpu as pltpu
from jax.sharding import PartitionSpec as P

BF = jnp.bfloat16
F32 = jnp.float32
HIGHEST = lax.Precision.HIGHEST
NT = (((1,), (1,)), ((), ()))
CHUNK = 512
X_SIZE = 4
RELATIVE = ((0, 0), (0, 1), (-1, 0), (-1, 1), (1, 0), (1, 1), (2, 0), (2, 1))
EARLY, LATE = (7, 6, 3, 5), (2, 4, 1, 0)
PARAMS = pltpu.CompilerParams(vmem_limit_bytes=60 * 1024 * 1024)
SMALL = pltpu.CompilerParams(vmem_limit_bytes=16 * 1024 * 1024)


def split2(x):
    hi = x.astype(BF)
    return hi, (x - hi.astype(F32)).astype(BF)


def mm(a, b):
    return jnp.dot(a, b, preferred_element_type=F32)


def mm_nt(a, b):
    return lax.dot_general(a, b, NT, preferred_element_type=F32)


def sigma(v):
    return 0.5 * jnp.tanh(0.5 * v) + 0.5


def wide(x):
    return jnp.concatenate(split2(x), axis=1)


def tall(x):
    return jnp.concatenate(split2(x), axis=0)


def twice(x):
    return jnp.concatenate([x, x], axis=0)


def chunks_of(width):
    return [slice(i, i + CHUNK) for i in range(0, width, CHUNK)]


def up_of(all_ref, cols):
    dp, rows, _ = all_ref.shape
    return all_ref[:, : rows // 2, cols].reshape(dp * rows // 2, -1)


def down_of(all_ref, cols):
    dp, rows, _ = all_ref.shape
    return all_ref[:, rows // 2 :, cols].reshape(dp * rows // 2, -1)


def gram_share(x, all_ref):
    rank = x.shape[1]
    cols = slice(all_ref.shape[2] - rank, all_ref.shape[2])
    gram = up_of(all_ref, cols).astype(F32) + down_of(all_ref, cols).astype(F32)
    return 0.25 * jnp.dot(x, gram, precision=HIGHEST, preferred_element_type=F32)


def first_kernel(base_ref, all_ref, part_ref):
    acc = jnp.zeros(part_ref.shape, F32)
    for cols in chunks_of(base_ref.shape[1]):
        pre = base_ref[:, cols].astype(F32)
        hidden = (pre * sigma(pre)).astype(BF)
        acc += mm_nt(hidden, down_of(all_ref, cols))
    part_ref[...] = acc


def forward_kernel(base_ref, all_ref, r0, r1, part_ref):
    c = r0[...] + r1[...]
    cw = wide(c)
    acc = gram_share(c, all_ref)
    for cols in chunks_of(base_ref.shape[1]):
        pre = base_ref[:, cols].astype(F32) + mm(cw, twice(up_of(all_ref, cols)))
        hidden = (pre * sigma(pre)).astype(BF)
        acc += mm_nt(hidden, down_of(all_ref, cols))
    part_ref[...] = acc


def middle_kernel(base_ref, all_ref, r0, r1, c_ref, part_ref, slope_ref):
    c = r0[...] + r1[...]
    c_ref[...] = c.astype(BF)
    cw = wide(c)
    acc = gram_share(c, all_ref)
    for cols in chunks_of(base_ref.shape[1]):
        pre = base_ref[:, cols].astype(F32) + mm(cw, twice(up_of(all_ref, cols)))
        sig = sigma(pre)
        hidden = (pre * sig).astype(BF)
        slope_ref[:, cols] = (sig * (1.0 + pre * (1.0 - sig))).astype(BF)
        acc += mm_nt(hidden, down_of(all_ref, cols))
    part_ref[...] = acc


def backward_kernel(last_ref, slope_ref, all_ref, cot_ref, r0, r1, part_ref):
    g = jnp.where(last_ref[0] == 1, cot_ref[...], r0[...] + r1[...])
    gw = wide(g)
    acc = gram_share(g, all_ref)
    for cols in chunks_of(slope_ref.shape[1]):
        g_pre = mm(gw, twice(down_of(all_ref, cols))) * slope_ref[:, cols].astype(F32)
        hi, lo = split2(g_pre)
        up = up_of(all_ref, cols)
        acc += mm_nt(hi, up) + mm_nt(lo, up)
    part_ref[...] = acc


def call(kernel, outs, *args):
    return pl.pallas_call(kernel, out_shape=outs, compiler_params=SMALL)(*args)


def base_specs(base, dp, blocks):
    micro, tokens, width = base.shape
    return [
        pl.BlockSpec((micro, tokens // dp, width), lambda i, p, j=j: (0, p[j], 0)) for j in blocks
    ]


def product_kernel(count, plan, place_ref, *refs):
    bases, w_ref, outs, rows = refs[:count], refs[count], refs[count + 1 : -1], refs[-1]
    own = bases[0].shape[0] * bases[0].shape[1]

    @pl.when(pl.program_id(0) == 0)
    def _():
        for j, b in enumerate(bases):
            rows[j * own : (j + 1) * own] = b[...].reshape(own, b.shape[2])

    res = mm(rows[...], w_ref[...])
    for out, parts in zip(outs, plan):
        start = 0
        for j, begin, end in parts:
            out[start : start + end - begin] = res[j * own + begin : j * own + end].astype(BF)
            start += end - begin


def product(place, base, w_in, dp, blocks, plan):
    micro, tokens, width = base.shape
    hid = w_in.shape[1]
    own = micro * tokens // dp
    count = len(blocks)
    heights = [sum(end - begin for _, begin, end in parts) for parts in plan]
    column = lambda rows: pl.BlockSpec((rows, CHUNK), lambda i, p: (0, i))
    return pl.pallas_call(
        functools.partial(product_kernel, count, plan),
        out_shape=[jax.ShapeDtypeStruct((rows, hid), BF) for rows in heights],
        grid_spec=pltpu.PrefetchScalarGridSpec(
            num_scalar_prefetch=1,
            grid=(hid // CHUNK,),
            in_specs=base_specs(base, dp, blocks) + [column(width)],
            out_specs=[column(rows) for rows in heights],
            scratch_shapes=[pltpu.VMEM((own * count, width), BF)],
        ),
        compiler_params=PARAMS,
    )(place, *([base] * count), w_in)


def project_kernel(basis_ref, w_in_ref, w_out_ref, out_ref, wide_ref, tall_ref):
    rank = basis_ref.shape[1]
    count, rows, cols = out_ref.shape
    share = rows // 2
    step = pl.program_id(0)

    @pl.when(step == 0)
    def _():
        basis = basis_ref[...]
        wide_ref[...] = wide(basis)
        tall_ref[...] = tall(basis.T)
        gram = jnp.dot(basis.T, basis, precision=HIGHEST, preferred_element_type=F32)
        hi, lo = split2(gram)
        out_ref[:, :share, cols - rank :] = hi.reshape(count, share, rank)
        out_ref[:, share:, cols - rank :] = lo.reshape(count, share, rank)

    here = pl.ds(pl.multiple_of(step * CHUNK, CHUNK), CHUNK)
    up = mm(tall_ref[...], w_in_ref[...])
    down = mm(w_out_ref[...], wide_ref[...])
    out_ref[:, :share, here] = (up[:rank] + up[rank:]).astype(BF).reshape(count, share, CHUNK)
    down = (down[:, :rank] + down[:, rank:]).T
    out_ref[:, share:, here] = down.astype(BF).reshape(count, share, CHUNK)


def project(basis, w_in, w_out, dp):
    width, rank = basis.shape
    hid = w_in.shape[1]
    shape = (dp, 2 * rank // dp, hid + rank)
    return pl.pallas_call(
        project_kernel,
        out_shape=jax.ShapeDtypeStruct(shape, BF),
        grid=(hid // CHUNK,),
        in_specs=[
            pl.BlockSpec((width, rank), lambda i: (0, 0)),
            pl.BlockSpec((width, CHUNK), lambda i: (0, i)),
            pl.BlockSpec((CHUNK, width), lambda i: (i, 0)),
        ],
        out_specs=pl.BlockSpec(shape, lambda i: (0, 0, 0)),
        scratch_shapes=[pltpu.VMEM((width, 2 * rank), BF), pltpu.VMEM((2 * rank, width), BF)],
        compiler_params=PARAMS,
    )(basis, w_in, w_out)


def fold_kernel(rank, x_ref, out_ref):
    count, rows, cols = x_ref.shape
    share = rows // 2
    total = x_ref[0].astype(F32)
    for d in range(1, count):
        total += x_ref[d].astype(F32)
    hi, lo = split2(total[:share, cols - rank :] + total[share:, cols - rank :])
    own = jnp.concatenate(
        [total[:, : cols - rank].astype(BF), jnp.concatenate([hi, lo], axis=0)], axis=1
    )
    for d in range(count):
        out_ref[d] = own


def turn_kernel(place_ref, *refs):
    bases, out = refs[:-1], refs[-1]
    own = bases[0].shape[0] * bases[0].shape[1]
    for j, b in enumerate(bases):
        rows = b[...].reshape(own, b.shape[2]).astype(F32)
        out[:, j * own : (j + 1) * own] = rows.T.astype(BF)


def turn(place, base, dp):
    micro, tokens, width = base.shape
    count = len(RELATIVE)
    shape = (width, micro * tokens)
    return pl.pallas_call(
        turn_kernel,
        out_shape=jax.ShapeDtypeStruct(shape, BF),
        grid_spec=pltpu.PrefetchScalarGridSpec(
            num_scalar_prefetch=1,
            grid=(1,),
            in_specs=base_specs(base, dp, range(count)),
            out_specs=pl.BlockSpec(shape, lambda i, p: (0, 0)),
        ),
        compiler_params=PARAMS,
    )(place, *([base] * count))


def finish_kernel(place_ref, ex_ref, all_ref, base_ref, basis_ref, *refs):
    pieces, (grad_ref, dc_ref, xt, gg, gt, cc, hidden, g_pre) = refs[:-8], refs[-8:]
    own, two = ex_ref.shape[1:]
    rank = two // 2

    @pl.when(pl.program_id(0) == 0)
    def _():
        basis = basis_ref[...].astype(BF)
        for j in range(len(RELATIVE)):
            ex = ex_ref[place_ref[j]]
            rows = slice(j * own, (j + 1) * own)
            g, c = ex[:, :rank], ex[:, rank:]
            gg[rows] = g
            cc[rows] = c
            gt[:, rows] = g.astype(F32).T.astype(BF)
            xt[:, rows] = (base_ref[:, rows].astype(F32) + mm_nt(basis, c)).astype(BF)

    every = slice(0, all_ref.shape[2])
    from_c = mm(cc[...], up_of(all_ref, every))
    g_hidden = mm(gg[...], down_of(all_ref, every))
    start = 0
    for p in pieces:
        rows = slice(start, start + p.shape[0])
        start += p.shape[0]
        pre = p[...].astype(F32) + from_c[rows]
        sig = sigma(pre)
        out = pre * sig
        hidden[rows] = out.astype(BF)
        g_pre[rows] = (g_hidden[rows] * (sig + out * (1.0 - sig))).astype(BF)
    grad_ref[...] = mm(xt[...], g_pre[...]).astype(BF)
    dc_ref[...] = mm(gt[...], hidden[...]).T


def finish(place, ex, everyone, base_t, basis, pieces):
    width, tokens = base_t.shape
    hid = pieces[0].shape[1]
    rank = basis.shape[1]
    dp, rows, _ = everyone.shape
    column = lambda rows: pl.BlockSpec((rows, CHUNK), lambda i, p: (0, i))
    return pl.pallas_call(
        finish_kernel,
        out_shape=[jax.ShapeDtypeStruct((width, hid), BF), jax.ShapeDtypeStruct((hid, rank), F32)],
        grid_spec=pltpu.PrefetchScalarGridSpec(
            num_scalar_prefetch=1,
            grid=(hid // CHUNK,),
            in_specs=[
                pl.BlockSpec(ex.shape, lambda i, p: (0, 0, 0)),
                pl.BlockSpec((dp, rows, CHUNK), lambda i, p: (0, 0, i)),
                pl.BlockSpec(base_t.shape, lambda i, p: (0, 0)),
                pl.BlockSpec(basis.shape, lambda i, p: (0, 0)),
            ]
            + [column(p.shape[0]) for p in pieces],
            out_specs=[column(width), pl.BlockSpec((CHUNK, rank), lambda i, p: (i, 0))],
            scratch_shapes=[
                pltpu.VMEM((width, tokens), BF),
                pltpu.VMEM((tokens, rank), BF),
                pltpu.VMEM((rank, tokens), BF),
                pltpu.VMEM((tokens, rank), BF),
                pltpu.VMEM((tokens, CHUNK), BF),
                pltpu.VMEM((tokens, CHUNK), BF),
            ],
        ),
        compiler_params=PARAMS,
    )(place, ex, everyone, base_t, basis, *pieces)


def to_dp(x, dx, dy):
    size = lax.axis_size("dp")
    pairs = [(i, ((i // 2 + dx) % X_SIZE) * 2 + ((i % 2) ^ dy)) for i in range(size)]
    return lax.ppermute(x, "dp", pairs)


def to_tensor(x, k):
    size = lax.axis_size("tensor")
    return lax.ppermute(x, "tensor", [(t, t ^ k) for t in range(size)])


def hop(part, by, before=(), during=lambda *a: ()):
    sections, tensors = lax.axis_size("section"), lax.axis_size("tensor")
    pair_sum, before = tie(part + to_tensor(part, 1), before)
    pairs = [
        (s * tensors + t, (s + by) * tensors + (t ^ (2 * (t % 2))))
        for s in range(sections)
        for t in range(tensors)
        if 0 <= s + by < sections
    ]
    got = lax.ppermute(pair_sum, ("section", "tensor"), pairs)
    got, made = tie(got, during(*before))
    return (got, to_tensor(got, 1)), before, made


def cat(*xs):
    return jnp.concatenate(xs, axis=0)


def plus(x, *ys):
    total = x.astype(F32)
    for start, y in ys:
        pads = ((start, x.shape[0] - start - y.shape[0]), (0, 0))
        total = total + jnp.pad(y.astype(F32), pads)
    return total.astype(x.dtype)


def reduce_2(two, left_1, right_1, steps):
    u0, u1, v = steps
    h, q = two.shape[0] // 2, two.shape[0] // 4
    up = cat(two[:h], plus(right_1, (0, u0)))
    down = cat(plus(two[h:], (0, v)), plus(left_1, (q, u1)))
    return up, down


def reduce_3(left, right, side, up, down, other):
    h = left.shape[0] // 2
    return (
        plus(right, (0, up[:h]), (h, other[:h])),
        plus(left, (h, down[:h]), (h, other[h:])),
        plus(side, (0, up[h:]), (0, down[h:])),
    )


def swap(x):
    return lax.all_to_all(x, "dp", 0, 0, tiled=True)


def tie(*xs):
    return lax.optimization_barrier(xs)


def on_device(base, w_in, w_out, basis, cotangent):
    dp = lax.axis_size("dp")
    sections = lax.axis_size("section")
    last = (lax.axis_index("section") == sections - 1).astype(jnp.int32).reshape(1)
    d = lax.axis_index("dp")
    place = jnp.stack(
        [((d // 2 + dx) % X_SIZE) * 2 + (d % 2 + dy) % 2 for dx, dy in RELATIVE]
    ).astype(jnp.int32)
    micro, tokens, width = base.shape
    rows = tokens // dp
    own = micro * rows
    rank = basis.shape[1]
    w_in, w_out = w_in[0], w_out[0]
    hid = w_in.shape[1]
    tok = jax.ShapeDtypeStruct((own, rank), F32)
    f = lambda a: a.astype(F32)

    h, q = own // 2, own // 4
    cuts = [
        [(0, 0, q)], [(0, q, h)], [(0, h, own)], [(1, 0, own)], [(2, 0, h)], [(3, 0, h)],
        [(3, h, own), (2, h, own)],
    ]
    early = product(place, base, w_in, dp, EARLY, cuts)
    (*far, two, left_1, right_1, other), base_1 = tie(early, base)
    steps = to_dp(far[0], 1, 0), to_dp(far[1], -1, 0), to_dp(far[2], 0, 1)
    base_t = turn(place, base_1, dp)
    steps, base_t = tie(steps, base_t)
    up, down = reduce_2(two, left_1, right_1, steps)
    up, down, other, basis_1 = tie(up, down, other, basis)
    up, down, other = to_dp(up, 1, 0), to_dp(down, -1, 0), to_dp(other, 0, 1)
    proj = project(basis_1, w_in, w_out, dp)
    up, down, other, proj, base_2 = tie(up, down, other, proj, base_1)
    proj = swap(proj)
    late = product(place, base_2, w_in, dp, LATE, [[(j, 0, own)] for j in range(len(LATE))])
    proj, late = tie(proj, late)
    proj = call(functools.partial(fold_kernel, rank), jax.ShapeDtypeStruct(proj.shape, BF), proj)
    everyone = swap(proj)
    left, right, side, mine = late
    sent = reduce_3(left, right, side, up, down, other)
    got = to_dp(sent[0], 1, 0), to_dp(sent[1], -1, 0), to_dp(sent[2], 0, 1)
    own_pre = ((f(mine) + f(got[0])) + (f(got[1]) + f(got[2]))).astype(BF)

    left, right = to_dp(own_pre, 1, 0), to_dp(own_pre, -1, 0)
    part = call(first_kernel, tok, own_pre, everyone)
    got, _, mine = hop(part, 1, (own_pre,), lambda a: (a[:h], a[h:]))
    side_low = to_dp(mine[0], 0, 1)
    part = call(forward_kernel, tok, own_pre, everyone, *got)
    got, _, _ = hop(part, 1)
    got, left, right, side_low, high = tie(got, left, right, side_low, mine[1])
    side_high = to_dp(high, 0, 1)
    far = to_dp(left, 1, 0)
    part = call(forward_kernel, tok, own_pre, everyone, *got)
    got, _, _ = hop(part, 1)
    got, side_low = tie(got, side_low)
    left_low, right_low = to_dp(side_low, 1, 0), to_dp(side_low, -1, 0)
    c_in, coef_part, slope = call(
        middle_kernel,
        (jax.ShapeDtypeStruct((own, rank), BF), tok, jax.ShapeDtypeStruct((own, hid), BF)),
        own_pre, everyone, *got,
    )
    cot = cotangent.reshape(own, rank)

    def back(got):
        return call(backward_kernel, tok, last, slope, everyone, cot, *got)

    got, _, _ = hop(back((cot, cot)), -1)
    got, far, side_high, left_low, right_low = tie(got, far, side_high, left_low, right_low)
    left_high, right_high = to_dp(side_high, 1, 0), to_dp(side_high, -1, 0)
    far_low = to_dp(left_low, 1, 0)
    got, _, _ = hop(back(got), -1)
    got, left_high, right_high = tie(got, left_high, right_high)
    far_high = to_dp(right_high, -1, 0)
    got, _, _ = hop(back(got), -1)
    got, far_low, far_high = tie(got, far_low, far_high)
    g_out = jnp.where(last[0] == 1, cot, got[0] + got[1])
    ex = jnp.concatenate([g_out.astype(BF), c_in], axis=1)
    ex = swap(jnp.broadcast_to(ex[None], (dp,) + ex.shape))
    parts = cat(coef_part, back(got))
    parts = parts + to_tensor(parts, 1)
    ex, parts = tie(ex, parts)
    pieces = [
        own_pre, side_low, side_high, left, left_low, left_high,
        right, right_low, right_high, far, far_low, far_high,
    ]
    grad_up, down_coefs = finish(place, ex, everyone, base_t, basis, pieces)
    parts = (parts + to_tensor(parts, 2)).reshape(2, 1, micro, rows, rank)
    return parts[0], parts[1], grad_up[None], down_coefs[None]


def solution(mesh):
    return jax.shard_map(
        on_device,
        mesh=mesh,
        in_specs=(
            P(None, None, "dp"),
            P("section", "dp", "tensor"),
            P("section", "tensor", "dp"),
            P("dp", None),
            P(None, "dp", None),
        ),
        out_specs=(
            P("section", None, "dp", None),
            P("section", None, "dp", None),
            P("section", "dp", "tensor"),
            P("section", "tensor", None),
        ),
        check_vma=False,
    )
```

```python
import functools

import jax
import jax.numpy as jnp
from jax import lax
from jax.experimental import pallas as pl
from jax.experimental.pallas import tpu as pltpu
from jax.sharding import PartitionSpec as P

BF = jnp.bfloat16
F32 = jnp.float32
HIGHEST = lax.Precision.HIGHEST
NT = (((1,), (1,)), ((), ()))
CHUNK = 512
X_SIZE = 4
RELATIVE = ((0, 0), (0, 1), (-1, 0), (-1, 1), (1, 0), (1, 1), (2, 0), (2, 1))
EARLY, LATE = (7, 6, 3, 5), (2, 4, 1, 0)
PARAMS = pltpu.CompilerParams(vmem_limit_bytes=60 * 1024 * 1024)
SMALL = pltpu.CompilerParams(vmem_limit_bytes=16 * 1024 * 1024)


def split2(x):
    hi = x.astype(BF)
    return hi, (x - hi.astype(F32)).astype(BF)


def mm(a, b):
    return jnp.dot(a, b, preferred_element_type=F32)


def mm_nt(a, b):
    return lax.dot_general(a, b, NT, preferred_element_type=F32)


def sigma(v):
    return 0.5 * jnp.tanh(0.5 * v) + 0.5


def wide(x):
    return jnp.concatenate(split2(x), axis=1)


def tall(x):
    return jnp.concatenate(split2(x), axis=0)


def twice(x):
    return jnp.concatenate([x, x], axis=0)


def chunks_of(width):
    return [slice(i, i + CHUNK) for i in range(0, width, CHUNK)]


def up_of(all_ref, cols):
    dp, rows, _ = all_ref.shape
    return all_ref[:, : rows // 2, cols].reshape(dp * rows // 2, -1)


def down_of(all_ref, cols):
    dp, rows, _ = all_ref.shape
    return all_ref[:, rows // 2 :, cols].reshape(dp * rows // 2, -1)


def gram_share(x, all_ref):
    rank = x.shape[1]
    cols = slice(all_ref.shape[2] - rank, all_ref.shape[2])
    gram = up_of(all_ref, cols).astype(F32) + down_of(all_ref, cols).astype(F32)
    return 0.25 * jnp.dot(x, gram, precision=HIGHEST, preferred_element_type=F32)


def first_kernel(base_ref, all_ref, part_ref):
    acc = jnp.zeros(part_ref.shape, F32)
    for cols in chunks_of(base_ref.shape[1]):
        pre = base_ref[:, cols].astype(F32)
        hidden = (pre * sigma(pre)).astype(BF)
        acc += mm_nt(hidden, down_of(all_ref, cols))
    part_ref[...] = acc


def forward_kernel(base_ref, all_ref, r0, r1, part_ref):
    c = r0[...] + r1[...]
    cw = wide(c)
    acc = gram_share(c, all_ref)
    for cols in chunks_of(base_ref.shape[1]):
        pre = base_ref[:, cols].astype(F32) + mm(cw, twice(up_of(all_ref, cols)))
        hidden = (pre * sigma(pre)).astype(BF)
        acc += mm_nt(hidden, down_of(all_ref, cols))
    part_ref[...] = acc


def middle_kernel(base_ref, all_ref, r0, r1, c_ref, part_ref, slope_ref):
    c = r0[...] + r1[...]
    c_ref[...] = c.astype(BF)
    cw = wide(c)
    acc = gram_share(c, all_ref)
    for cols in chunks_of(base_ref.shape[1]):
        pre = base_ref[:, cols].astype(F32) + mm(cw, twice(up_of(all_ref, cols)))
        sig = sigma(pre)
        hidden = (pre * sig).astype(BF)
        slope_ref[:, cols] = (sig * (1.0 + pre * (1.0 - sig))).astype(BF)
        acc += mm_nt(hidden, down_of(all_ref, cols))
    part_ref[...] = acc


def backward_kernel(last_ref, slope_ref, all_ref, cot_ref, r0, r1, part_ref):
    g = jnp.where(last_ref[0] == 1, cot_ref[...], r0[...] + r1[...])
    gw = wide(g)
    acc = gram_share(g, all_ref)
    for cols in chunks_of(slope_ref.shape[1]):
        g_pre = mm(gw, twice(down_of(all_ref, cols))) * slope_ref[:, cols].astype(F32)
        hi, lo = split2(g_pre)
        up = up_of(all_ref, cols)
        acc += mm_nt(hi, up) + mm_nt(lo, up)
    part_ref[...] = acc


def call(kernel, outs, *args):
    return pl.pallas_call(kernel, out_shape=outs, compiler_params=SMALL)(*args)


def base_specs(base, dp, blocks):
    micro, tokens, width = base.shape
    return [
        pl.BlockSpec((micro, tokens // dp, width), lambda i, p, j=j: (0, p[j], 0)) for j in blocks
    ]


def product_kernel(count, plan, place_ref, *refs):
    bases, w_ref, outs, rows = refs[:count], refs[count], refs[count + 1 : -1], refs[-1]
    own = bases[0].shape[0] * bases[0].shape[1]

    @pl.when(pl.program_id(0) == 0)
    def _():
        for j, b in enumerate(bases):
            rows[j * own : (j + 1) * own] = b[...].reshape(own, b.shape[2])

    res = mm(rows[...], w_ref[...])
    for out, parts in zip(outs, plan):
        start = 0
        for j, begin, end in parts:
            out[start : start + end - begin] = res[j * own + begin : j * own + end].astype(BF)
            start += end - begin


def product(place, base, w_in, dp, blocks, plan):
    micro, tokens, width = base.shape
    hid = w_in.shape[1]
    own = micro * tokens // dp
    count = len(blocks)
    heights = [sum(end - begin for _, begin, end in parts) for parts in plan]
    column = lambda rows: pl.BlockSpec((rows, CHUNK), lambda i, p: (0, i))
    return pl.pallas_call(
        functools.partial(product_kernel, count, plan),
        out_shape=[jax.ShapeDtypeStruct((rows, hid), BF) for rows in heights],
        grid_spec=pltpu.PrefetchScalarGridSpec(
            num_scalar_prefetch=1,
            grid=(hid // CHUNK,),
            in_specs=base_specs(base, dp, blocks) + [column(width)],
            out_specs=[column(rows) for rows in heights],
            scratch_shapes=[pltpu.VMEM((own * count, width), BF)],
        ),
        compiler_params=PARAMS,
    )(place, *([base] * count), w_in)


def project_kernel(basis_ref, w_in_ref, w_out_ref, out_ref, wide_ref, tall_ref):
    rank = basis_ref.shape[1]
    count, rows, cols = out_ref.shape
    share = rows // 2
    step = pl.program_id(0)

    @pl.when(step == 0)
    def _():
        basis = basis_ref[...]
        wide_ref[...] = wide(basis)
        tall_ref[...] = tall(basis.T)
        gram = jnp.dot(basis.T, basis, precision=HIGHEST, preferred_element_type=F32)
        hi, lo = split2(gram)
        out_ref[:, :share, cols - rank :] = hi.reshape(count, share, rank)
        out_ref[:, share:, cols - rank :] = lo.reshape(count, share, rank)

    here = pl.ds(pl.multiple_of(step * CHUNK, CHUNK), CHUNK)
    up = mm(tall_ref[...], w_in_ref[...])
    down = mm(w_out_ref[...], wide_ref[...])
    out_ref[:, :share, here] = (up[:rank] + up[rank:]).astype(BF).reshape(count, share, CHUNK)
    down = (down[:, :rank] + down[:, rank:]).T
    out_ref[:, share:, here] = down.astype(BF).reshape(count, share, CHUNK)


def project(basis, w_in, w_out, dp):
    width, rank = basis.shape
    hid = w_in.shape[1]
    shape = (dp, 2 * rank // dp, hid + rank)
    return pl.pallas_call(
        project_kernel,
        out_shape=jax.ShapeDtypeStruct(shape, BF),
        grid=(hid // CHUNK,),
        in_specs=[
            pl.BlockSpec((width, rank), lambda i: (0, 0)),
            pl.BlockSpec((width, CHUNK), lambda i: (0, i)),
            pl.BlockSpec((CHUNK, width), lambda i: (i, 0)),
        ],
        out_specs=pl.BlockSpec(shape, lambda i: (0, 0, 0)),
        scratch_shapes=[pltpu.VMEM((width, 2 * rank), BF), pltpu.VMEM((2 * rank, width), BF)],
        compiler_params=PARAMS,
    )(basis, w_in, w_out)


def fold_kernel(rank, x_ref, out_ref):
    count, rows, cols = x_ref.shape
    share = rows // 2
    total = x_ref[0].astype(F32)
    for d in range(1, count):
        total += x_ref[d].astype(F32)
    hi, lo = split2(total[:share, cols - rank :] + total[share:, cols - rank :])
    own = jnp.concatenate(
        [total[:, : cols - rank].astype(BF), jnp.concatenate([hi, lo], axis=0)], axis=1
    )
    for d in range(count):
        out_ref[d] = own


def turn_kernel(place_ref, *refs):
    bases, out = refs[:-1], refs[-1]
    own = bases[0].shape[0] * bases[0].shape[1]
    for j, b in enumerate(bases):
        rows = b[...].reshape(own, b.shape[2]).astype(F32)
        out[:, j * own : (j + 1) * own] = rows.T.astype(BF)


def turn(place, base, dp):
    micro, tokens, width = base.shape
    count = len(RELATIVE)
    shape = (width, micro * tokens)
    return pl.pallas_call(
        turn_kernel,
        out_shape=jax.ShapeDtypeStruct(shape, BF),
        grid_spec=pltpu.PrefetchScalarGridSpec(
            num_scalar_prefetch=1,
            grid=(1,),
            in_specs=base_specs(base, dp, range(count)),
            out_specs=pl.BlockSpec(shape, lambda i, p: (0, 0)),
        ),
        compiler_params=PARAMS,
    )(place, *([base] * count))


def finish_kernel(place_ref, ex_ref, all_ref, base_ref, basis_ref, *refs):
    pieces, (grad_ref, dc_ref, xt, gg, gt, cc, hidden, g_pre) = refs[:-8], refs[-8:]
    own, two = ex_ref.shape[1:]
    rank = two // 2

    @pl.when(pl.program_id(0) == 0)
    def _():
        basis = basis_ref[...].astype(BF)
        for j in range(len(RELATIVE)):
            ex = ex_ref[place_ref[j]]
            rows = slice(j * own, (j + 1) * own)
            g, c = ex[:, :rank], ex[:, rank:]
            gg[rows] = g
            cc[rows] = c
            gt[:, rows] = g.astype(F32).T.astype(BF)
            xt[:, rows] = (base_ref[:, rows].astype(F32) + mm_nt(basis, c)).astype(BF)

    every = slice(0, all_ref.shape[2])
    from_c = mm(cc[...], up_of(all_ref, every))
    g_hidden = mm(gg[...], down_of(all_ref, every))
    start = 0
    for p in pieces:
        rows = slice(start, start + p.shape[0])
        start += p.shape[0]
        pre = p[...].astype(F32) + from_c[rows]
        sig = sigma(pre)
        out = pre * sig
        hidden[rows] = out.astype(BF)
        g_pre[rows] = (g_hidden[rows] * (sig + out * (1.0 - sig))).astype(BF)
    grad_ref[...] = mm(xt[...], g_pre[...]).astype(BF)
    dc_ref[...] = mm(gt[...], hidden[...]).T


def finish(place, ex, everyone, base_t, basis, pieces):
    width, tokens = base_t.shape
    hid = pieces[0].shape[1]
    rank = basis.shape[1]
    dp, rows, _ = everyone.shape
    column = lambda rows: pl.BlockSpec((rows, CHUNK), lambda i, p: (0, i))
    return pl.pallas_call(
        finish_kernel,
        out_shape=[jax.ShapeDtypeStruct((width, hid), BF), jax.ShapeDtypeStruct((hid, rank), F32)],
        grid_spec=pltpu.PrefetchScalarGridSpec(
            num_scalar_prefetch=1,
            grid=(hid // CHUNK,),
            in_specs=[
                pl.BlockSpec(ex.shape, lambda i, p: (0, 0, 0)),
                pl.BlockSpec((dp, rows, CHUNK), lambda i, p: (0, 0, i)),
                pl.BlockSpec(base_t.shape, lambda i, p: (0, 0)),
                pl.BlockSpec(basis.shape, lambda i, p: (0, 0)),
            ]
            + [column(p.shape[0]) for p in pieces],
            out_specs=[column(width), pl.BlockSpec((CHUNK, rank), lambda i, p: (i, 0))],
            scratch_shapes=[
                pltpu.VMEM((width, tokens), BF),
                pltpu.VMEM((tokens, rank), BF),
                pltpu.VMEM((rank, tokens), BF),
                pltpu.VMEM((tokens, rank), BF),
                pltpu.VMEM((tokens, CHUNK), BF),
                pltpu.VMEM((tokens, CHUNK), BF),
            ],
        ),
        compiler_params=PARAMS,
    )(place, ex, everyone, base_t, basis, *pieces)


def to_dp(x, dx, dy):
    size = lax.axis_size("dp")
    pairs = [(i, ((i // 2 + dx) % X_SIZE) * 2 + ((i % 2) ^ dy)) for i in range(size)]
    return lax.ppermute(x, "dp", pairs)


def to_tensor(x, k):
    size = lax.axis_size("tensor")
    return lax.ppermute(x, "tensor", [(t, t ^ k) for t in range(size)])


def hop(part, by, before=(), during=lambda *a: ()):
    sections, tensors = lax.axis_size("section"), lax.axis_size("tensor")
    pair_sum, before = tie(part + to_tensor(part, 1), before)
    pairs = [
        (s * tensors + t, (s + by) * tensors + (t ^ (2 * (t % 2))))
        for s in range(sections)
        for t in range(tensors)
        if 0 <= s + by < sections
    ]
    got = lax.ppermute(pair_sum, ("section", "tensor"), pairs)
    got, made = tie(got, during(*before))
    return (got, to_tensor(got, 1)), before, made


def cat(*xs):
    return jnp.concatenate(xs, axis=0)


def plus(x, *ys):
    total = x.astype(F32)
    for start, y in ys:
        pads = ((start, x.shape[0] - start - y.shape[0]), (0, 0))
        total = total + jnp.pad(y.astype(F32), pads)
    return total.astype(x.dtype)


def reduce_2(two, left_1, right_1, steps):
    u0, u1, v = steps
    h, q = two.shape[0] // 2, two.shape[0] // 4
    up = cat(two[:h], plus(right_1, (0, u0)))
    down = cat(plus(two[h:], (0, v)), plus(left_1, (q, u1)))
    return up, down


def reduce_3(left, right, side, up, down, other):
    h = left.shape[0] // 2
    return (
        plus(right, (0, up[:h]), (h, other[:h])),
        plus(left, (h, down[:h]), (h, other[h:])),
        plus(side, (0, up[h:]), (0, down[h:])),
    )


def swap(x):
    return lax.all_to_all(x, "dp", 0, 0, tiled=True)


def tie(*xs):
    return lax.optimization_barrier(xs)


def on_device(base, w_in, w_out, basis, cotangent):
    dp = lax.axis_size("dp")
    sections = lax.axis_size("section")
    last = (lax.axis_index("section") == sections - 1).astype(jnp.int32).reshape(1)
    d = lax.axis_index("dp")
    place = jnp.stack(
        [((d // 2 + dx) % X_SIZE) * 2 + (d % 2 + dy) % 2 for dx, dy in RELATIVE]
    ).astype(jnp.int32)
    micro, tokens, width = base.shape
    rows = tokens // dp
    own = micro * rows
    rank = basis.shape[1]
    w_in, w_out = w_in[0], w_out[0]
    hid = w_in.shape[1]
    tok = jax.ShapeDtypeStruct((own, rank), F32)
    f = lambda a: a.astype(F32)

    h, q = own // 2, own // 4
    cuts = [
        [(0, 0, q)], [(0, q, h)], [(0, h, own)], [(1, 0, own)], [(2, 0, h)], [(3, 0, h)],
        [(3, h, own), (2, h, own)],
    ]
    early = product(place, base, w_in, dp, EARLY, cuts)
    (*far, two, left_1, right_1, other), base_1 = tie(early, base)
    steps = to_dp(far[0], 1, 0), to_dp(far[1], -1, 0), to_dp(far[2], 0, 1)
    base_t = turn(place, base_1, dp)
    steps, base_t = tie(steps, base_t)
    up, down = reduce_2(two, left_1, right_1, steps)
    up, down, other, basis_1 = tie(up, down, other, basis)
    up, down, other = to_dp(up, 1, 0), to_dp(down, -1, 0), to_dp(other, 0, 1)
    proj = project(basis_1, w_in, w_out, dp)
    up, down, base_2 = tie(up, down, base_1)
    proj = swap(proj)
    late = product(place, base_2, w_in, dp, LATE, [[(j, 0, own)] for j in range(len(LATE))])
    proj = call(functools.partial(fold_kernel, rank), jax.ShapeDtypeStruct(proj.shape, BF), proj)
    everyone = swap(proj)
    left, right, side, mine = late
    sent = reduce_3(left, right, side, up, down, other)
    got = to_dp(sent[0], 1, 0), to_dp(sent[1], -1, 0), to_dp(sent[2], 0, 1)
    own_pre = ((f(mine) + f(got[0])) + (f(got[1]) + f(got[2]))).astype(BF)

    left, right = to_dp(own_pre, 1, 0), to_dp(own_pre, -1, 0)
    part = call(first_kernel, tok, own_pre, everyone)
    got, _, mine = hop(part, 1, (own_pre,), lambda a: (a[:h], a[h:]))
    side_low = to_dp(mine[0], 0, 1)
    part = call(forward_kernel, tok, own_pre, everyone, *got)
    got, _, _ = hop(part, 1)
    got, left, right, side_low, high = tie(got, left, right, side_low, mine[1])
    side_high = to_dp(high, 0, 1)
    far_0, far_1 = to_dp(left[:h], 1, 0), to_dp(right[h:], -1, 0)
    part = call(forward_kernel, tok, own_pre, everyone, *got)
    got, _, _ = hop(part, 1)
    got, far_0, far_1 = tie(got, far_0, far_1)
    left_low, right_low = to_dp(side_low, 1, 0), to_dp(side_low, -1, 0)
    c_in, coef_part, slope = call(
        middle_kernel,
        (jax.ShapeDtypeStruct((own, rank), BF), tok, jax.ShapeDtypeStruct((own, hid), BF)),
        own_pre, everyone, *got,
    )
    cot = cotangent.reshape(own, rank)

    def back(got):
        return call(backward_kernel, tok, last, slope, everyone, cot, *got)

    got, _, _ = hop(back((cot, cot)), -1)
    got, side_high, left_low, right_low = tie(got, side_high, left_low, right_low)
    left_high, right_high = to_dp(side_high, 1, 0), to_dp(side_high, -1, 0)
    far_low = to_dp(left_low, 1, 0)
    got, _, _ = hop(back(got), -1)
    got, left_high, right_high = tie(got, left_high, right_high)
    far_high = to_dp(right_high, -1, 0)
    got, _, _ = hop(back(got), -1)
    got, far_low, far_high = tie(got, far_low, far_high)
    g_out = jnp.where(last[0] == 1, cot, got[0] + got[1])
    ex = jnp.concatenate([g_out.astype(BF), c_in], axis=1)
    ex = swap(jnp.broadcast_to(ex[None], (dp,) + ex.shape))
    parts = cat(coef_part, back(got))
    parts = parts + to_tensor(parts, 1)
    ex, parts = tie(ex, parts)
    pieces = [
        own_pre, side_low, side_high, left, left_low, left_high,
        right, right_low, right_high, far_0, far_1, far_low, far_high,
    ]
    grad_up, down_coefs = finish(place, ex, everyone, base_t, basis, pieces)
    parts = (parts + to_tensor(parts, 2)).reshape(2, 1, micro, rows, rank)
    return parts[0], parts[1], grad_up[None], down_coefs[None]


def solution(mesh):
    return jax.shard_map(
        on_device,
        mesh=mesh,
        in_specs=(
            P(None, None, "dp"),
            P("section", "dp", "tensor"),
            P("section", "tensor", "dp"),
            P("dp", None),
            P(None, "dp", None),
        ),
        out_specs=(
            P("section", None, "dp", None),
            P("section", None, "dp", None),
            P("section", "dp", "tensor"),
            P("section", "tensor", None),
        ),
        check_vma=False,
    )
```

```python
import functools

import jax
import jax.numpy as jnp
from jax import lax
from jax.experimental import pallas as pl
from jax.experimental.pallas import tpu as pltpu
from jax.sharding import PartitionSpec as P

BF = jnp.bfloat16
F32 = jnp.float32
HIGHEST = lax.Precision.HIGHEST
NT = (((1,), (1,)), ((), ()))
CHUNK = 512
X_SIZE = 4
RELATIVE = ((0, 0), (0, 1), (-1, 0), (-1, 1), (1, 0), (1, 1), (2, 0), (2, 1))
EARLY, LATE = (7, 6, 3, 5), (2, 4, 1, 0)
PARAMS = pltpu.CompilerParams(vmem_limit_bytes=60 * 1024 * 1024)
SMALL = pltpu.CompilerParams(vmem_limit_bytes=16 * 1024 * 1024)


def split2(x):
    hi = x.astype(BF)
    return hi, (x - hi.astype(F32)).astype(BF)


def mm(a, b):
    return jnp.dot(a, b, preferred_element_type=F32)


def mm_nt(a, b):
    return lax.dot_general(a, b, NT, preferred_element_type=F32)


def sigma(v):
    return 0.5 * jnp.tanh(0.5 * v) + 0.5


def wide(x):
    return jnp.concatenate(split2(x), axis=1)


def tall(x):
    return jnp.concatenate(split2(x), axis=0)


def twice(x):
    return jnp.concatenate([x, x], axis=0)


def chunks_of(width):
    return [slice(i, i + CHUNK) for i in range(0, width, CHUNK)]


def up_of(all_ref, cols):
    dp, rows, _ = all_ref.shape
    return all_ref[:, : rows // 2, cols].reshape(dp * rows // 2, -1)


def down_of(all_ref, cols):
    dp, rows, _ = all_ref.shape
    return all_ref[:, rows // 2 :, cols].reshape(dp * rows // 2, -1)


def gram_share(x, all_ref):
    rank = x.shape[1]
    cols = slice(all_ref.shape[2] - rank, all_ref.shape[2])
    gram = up_of(all_ref, cols).astype(F32) + down_of(all_ref, cols).astype(F32)
    return 0.25 * jnp.dot(x, gram, precision=HIGHEST, preferred_element_type=F32)


def first_kernel(base_ref, all_ref, part_ref):
    acc = jnp.zeros(part_ref.shape, F32)
    for cols in chunks_of(base_ref.shape[1]):
        pre = base_ref[:, cols].astype(F32)
        hidden = (pre * sigma(pre)).astype(BF)
        acc += mm_nt(hidden, down_of(all_ref, cols))
    part_ref[...] = acc


def forward_kernel(base_ref, all_ref, r0, r1, part_ref):
    c = r0[...] + r1[...]
    cw = wide(c)
    acc = gram_share(c, all_ref)
    for cols in chunks_of(base_ref.shape[1]):
        pre = base_ref[:, cols].astype(F32) + mm(cw, twice(up_of(all_ref, cols)))
        hidden = (pre * sigma(pre)).astype(BF)
        acc += mm_nt(hidden, down_of(all_ref, cols))
    part_ref[...] = acc


def middle_kernel(base_ref, all_ref, r0, r1, c_ref, part_ref, slope_ref):
    c = r0[...] + r1[...]
    c_ref[...] = c.astype(BF)
    cw = wide(c)
    acc = gram_share(c, all_ref)
    for cols in chunks_of(base_ref.shape[1]):
        pre = base_ref[:, cols].astype(F32) + mm(cw, twice(up_of(all_ref, cols)))
        sig = sigma(pre)
        hidden = (pre * sig).astype(BF)
        slope_ref[:, cols] = (sig * (1.0 + pre * (1.0 - sig))).astype(BF)
        acc += mm_nt(hidden, down_of(all_ref, cols))
    part_ref[...] = acc


def backward_kernel(last_ref, slope_ref, all_ref, cot_ref, r0, r1, part_ref):
    g = jnp.where(last_ref[0] == 1, cot_ref[...], r0[...] + r1[...])
    gw = wide(g)
    acc = gram_share(g, all_ref)
    for cols in chunks_of(slope_ref.shape[1]):
        g_pre = mm(gw, twice(down_of(all_ref, cols))) * slope_ref[:, cols].astype(F32)
        acc += mm_nt(g_pre.astype(BF), up_of(all_ref, cols))
    part_ref[...] = acc


def call(kernel, outs, *args):
    return pl.pallas_call(kernel, out_shape=outs, compiler_params=SMALL)(*args)


def base_specs(base, dp, blocks):
    micro, tokens, width = base.shape
    return [
        pl.BlockSpec((micro, tokens // dp, width), lambda i, p, j=j: (0, p[j], 0)) for j in blocks
    ]


def product_kernel(count, plan, place_ref, *refs):
    bases, w_ref, outs, rows = refs[:count], refs[count], refs[count + 1 : -1], refs[-1]
    own = bases[0].shape[0] * bases[0].shape[1]

    @pl.when(pl.program_id(0) == 0)
    def _():
        for j, b in enumerate(bases):
            rows[j * own : (j + 1) * own] = b[...].reshape(own, b.shape[2])

    res = mm(rows[...], w_ref[...])
    for out, parts in zip(outs, plan):
        start = 0
        for j, begin, end in parts:
            out[start : start + end - begin] = res[j * own + begin : j * own + end].astype(BF)
            start += end - begin


def product(place, base, w_in, dp, blocks, plan):
    micro, tokens, width = base.shape
    hid = w_in.shape[1]
    own = micro * tokens // dp
    count = len(blocks)
    heights = [sum(end - begin for _, begin, end in parts) for parts in plan]
    column = lambda rows: pl.BlockSpec((rows, CHUNK), lambda i, p: (0, i))
    return pl.pallas_call(
        functools.partial(product_kernel, count, plan),
        out_shape=[jax.ShapeDtypeStruct((rows, hid), BF) for rows in heights],
        grid_spec=pltpu.PrefetchScalarGridSpec(
            num_scalar_prefetch=1,
            grid=(hid // CHUNK,),
            in_specs=base_specs(base, dp, blocks) + [column(width)],
            out_specs=[column(rows) for rows in heights],
            scratch_shapes=[pltpu.VMEM((own * count, width), BF)],
        ),
        compiler_params=PARAMS,
    )(place, *([base] * count), w_in)


def project_kernel(basis_ref, w_in_ref, w_out_ref, out_ref, wide_ref, tall_ref):
    rank = basis_ref.shape[1]
    count, rows, cols = out_ref.shape
    share = rows // 2
    step = pl.program_id(0)

    @pl.when(step == 0)
    def _():
        basis = basis_ref[...]
        wide_ref[...] = wide(basis)
        tall_ref[...] = tall(basis.T)
        gram = jnp.dot(basis.T, basis, precision=HIGHEST, preferred_element_type=F32)
        hi, lo = split2(gram)
        out_ref[:, :share, cols - rank :] = hi.reshape(count, share, rank)
        out_ref[:, share:, cols - rank :] = lo.reshape(count, share, rank)

    here = pl.ds(pl.multiple_of(step * CHUNK, CHUNK), CHUNK)
    up = mm(tall_ref[...], w_in_ref[...])
    down = mm(w_out_ref[...], wide_ref[...])
    out_ref[:, :share, here] = (up[:rank] + up[rank:]).astype(BF).reshape(count, share, CHUNK)
    down = (down[:, :rank] + down[:, rank:]).T
    out_ref[:, share:, here] = down.astype(BF).reshape(count, share, CHUNK)


def project(basis, w_in, w_out, dp):
    width, rank = basis.shape
    hid = w_in.shape[1]
    shape = (dp, 2 * rank // dp, hid + rank)
    return pl.pallas_call(
        project_kernel,
        out_shape=jax.ShapeDtypeStruct(shape, BF),
        grid=(hid // CHUNK,),
        in_specs=[
            pl.BlockSpec((width, rank), lambda i: (0, 0)),
            pl.BlockSpec((width, CHUNK), lambda i: (0, i)),
            pl.BlockSpec((CHUNK, width), lambda i: (i, 0)),
        ],
        out_specs=pl.BlockSpec(shape, lambda i: (0, 0, 0)),
        scratch_shapes=[pltpu.VMEM((width, 2 * rank), BF), pltpu.VMEM((2 * rank, width), BF)],
        compiler_params=PARAMS,
    )(basis, w_in, w_out)


def fold_kernel(rank, x_ref, out_ref):
    count, rows, cols = x_ref.shape
    share = rows // 2
    total = x_ref[0].astype(F32)
    for d in range(1, count):
        total += x_ref[d].astype(F32)
    hi, lo = split2(total[:share, cols - rank :] + total[share:, cols - rank :])
    own = jnp.concatenate(
        [total[:, : cols - rank].astype(BF), jnp.concatenate([hi, lo], axis=0)], axis=1
    )
    for d in range(count):
        out_ref[d] = own


def turn_kernel(place_ref, *refs):
    bases, out = refs[:-1], refs[-1]
    own = bases[0].shape[0] * bases[0].shape[1]
    for j, b in enumerate(bases):
        rows = b[...].reshape(own, b.shape[2]).astype(F32)
        out[:, j * own : (j + 1) * own] = rows.T.astype(BF)


def turn(place, base, dp):
    micro, tokens, width = base.shape
    count = len(RELATIVE)
    shape = (width, micro * tokens)
    return pl.pallas_call(
        turn_kernel,
        out_shape=jax.ShapeDtypeStruct(shape, BF),
        grid_spec=pltpu.PrefetchScalarGridSpec(
            num_scalar_prefetch=1,
            grid=(1,),
            in_specs=base_specs(base, dp, range(count)),
            out_specs=pl.BlockSpec(shape, lambda i, p: (0, 0)),
        ),
        compiler_params=PARAMS,
    )(place, *([base] * count))


def finish_kernel(place_ref, ex_ref, all_ref, base_ref, basis_ref, *refs):
    pieces, (grad_ref, dc_ref, xt, gg, gt, cc, hidden, g_pre) = refs[:-8], refs[-8:]
    own, two = ex_ref.shape[1:]
    rank = two // 2

    @pl.when(pl.program_id(0) == 0)
    def _():
        basis = basis_ref[...].astype(BF)
        for j in range(len(RELATIVE)):
            ex = ex_ref[place_ref[j]]
            rows = slice(j * own, (j + 1) * own)
            g, c = ex[:, :rank], ex[:, rank:]
            gg[rows] = g
            cc[rows] = c
            gt[:, rows] = g.astype(F32).T.astype(BF)
            xt[:, rows] = (base_ref[:, rows].astype(F32) + mm_nt(basis, c)).astype(BF)

    every = slice(0, all_ref.shape[2])
    from_c = mm(cc[...], up_of(all_ref, every))
    g_hidden = mm(gg[...], down_of(all_ref, every))
    start = 0
    for p in pieces:
        rows = slice(start, start + p.shape[0])
        start += p.shape[0]
        pre = p[...].astype(F32) + from_c[rows]
        sig = sigma(pre)
        out = pre * sig
        hidden[rows] = out.astype(BF)
        g_pre[rows] = (g_hidden[rows] * (sig + out * (1.0 - sig))).astype(BF)
    grad_ref[...] = mm(xt[...], g_pre[...]).astype(BF)
    dc_ref[...] = mm(gt[...], hidden[...]).T


def finish(place, ex, everyone, base_t, basis, pieces):
    width, tokens = base_t.shape
    hid = pieces[0].shape[1]
    rank = basis.shape[1]
    dp, rows, _ = everyone.shape
    column = lambda rows: pl.BlockSpec((rows, CHUNK), lambda i, p: (0, i))
    return pl.pallas_call(
        finish_kernel,
        out_shape=[jax.ShapeDtypeStruct((width, hid), BF), jax.ShapeDtypeStruct((hid, rank), F32)],
        grid_spec=pltpu.PrefetchScalarGridSpec(
            num_scalar_prefetch=1,
            grid=(hid // CHUNK,),
            in_specs=[
                pl.BlockSpec(ex.shape, lambda i, p: (0, 0, 0)),
                pl.BlockSpec((dp, rows, CHUNK), lambda i, p: (0, 0, i)),
                pl.BlockSpec(base_t.shape, lambda i, p: (0, 0)),
                pl.BlockSpec(basis.shape, lambda i, p: (0, 0)),
            ]
            + [column(p.shape[0]) for p in pieces],
            out_specs=[column(width), pl.BlockSpec((CHUNK, rank), lambda i, p: (i, 0))],
            scratch_shapes=[
                pltpu.VMEM((width, tokens), BF),
                pltpu.VMEM((tokens, rank), BF),
                pltpu.VMEM((rank, tokens), BF),
                pltpu.VMEM((tokens, rank), BF),
                pltpu.VMEM((tokens, CHUNK), BF),
                pltpu.VMEM((tokens, CHUNK), BF),
            ],
        ),
        compiler_params=PARAMS,
    )(place, ex, everyone, base_t, basis, *pieces)


def to_dp(x, dx, dy):
    size = lax.axis_size("dp")
    pairs = [(i, ((i // 2 + dx) % X_SIZE) * 2 + ((i % 2) ^ dy)) for i in range(size)]
    return lax.ppermute(x, "dp", pairs)


def to_tensor(x, k):
    size = lax.axis_size("tensor")
    return lax.ppermute(x, "tensor", [(t, t ^ k) for t in range(size)])


def hop(part, by, before=(), during=lambda *a: ()):
    sections, tensors = lax.axis_size("section"), lax.axis_size("tensor")
    pair_sum, before = tie(part + to_tensor(part, 1), before)
    pairs = [
        (s * tensors + t, (s + by) * tensors + (t ^ (2 * (t % 2))))
        for s in range(sections)
        for t in range(tensors)
        if 0 <= s + by < sections
    ]
    got = lax.ppermute(pair_sum, ("section", "tensor"), pairs)
    got, made = tie(got, during(*before))
    return (got, to_tensor(got, 1)), before, made


def cat(*xs):
    return jnp.concatenate(xs, axis=0)


def plus(x, *ys):
    total = x.astype(F32)
    for start, y in ys:
        pads = ((start, x.shape[0] - start - y.shape[0]), (0, 0))
        total = total + jnp.pad(y.astype(F32), pads)
    return total.astype(x.dtype)


def reduce_2(two, left_1, right_1, steps):
    u0, u1, v = steps
    h, q = two.shape[0] // 2, two.shape[0] // 4
    up = cat(two[:h], plus(right_1, (0, u0)))
    down = cat(plus(two[h:], (0, v)), plus(left_1, (q, u1)))
    return up, down


def reduce_3(left, right, side, up, down, other):
    h = left.shape[0] // 2
    return (
        plus(right, (0, up[:h]), (h, other[:h])),
        plus(left, (h, down[:h]), (h, other[h:])),
        plus(side, (0, up[h:]), (0, down[h:])),
    )


def swap(x):
    return lax.all_to_all(x, "dp", 0, 0, tiled=True)


def tie(*xs):
    return lax.optimization_barrier(xs)


def on_device(base, w_in, w_out, basis, cotangent):
    dp = lax.axis_size("dp")
    sections = lax.axis_size("section")
    last = (lax.axis_index("section") == sections - 1).astype(jnp.int32).reshape(1)
    d = lax.axis_index("dp")
    place = jnp.stack(
        [((d // 2 + dx) % X_SIZE) * 2 + (d % 2 + dy) % 2 for dx, dy in RELATIVE]
    ).astype(jnp.int32)
    micro, tokens, width = base.shape
    rows = tokens // dp
    own = micro * rows
    rank = basis.shape[1]
    w_in, w_out = w_in[0], w_out[0]
    hid = w_in.shape[1]
    tok = jax.ShapeDtypeStruct((own, rank), F32)
    f = lambda a: a.astype(F32)

    h, q = own // 2, own // 4
    cuts = [
        [(0, 0, q)], [(0, q, h)], [(0, h, own)], [(1, 0, own)], [(2, 0, h)], [(3, 0, h)],
        [(3, h, own), (2, h, own)],
    ]
    early = product(place, base, w_in, dp, EARLY, cuts)
    (*far, two, left_1, right_1, other), base_1 = tie(early, base)
    steps = to_dp(far[0], 1, 0), to_dp(far[1], -1, 0), to_dp(far[2], 0, 1)
    base_t = turn(place, base_1, dp)
    steps, base_t = tie(steps, base_t)
    up, down = reduce_2(two, left_1, right_1, steps)
    up, down, basis_1 = tie(up, down, basis)
    up, down, other = to_dp(up, 1, 0), to_dp(down, -1, 0), to_dp(other, 0, 1)
    proj = project(basis_1, w_in, w_out, dp)
    up, down, base_2 = tie(up, down, base_1)
    proj = swap(proj)
    late = product(place, base_2, w_in, dp, LATE, [[(j, 0, own)] for j in range(len(LATE))])
    proj = call(functools.partial(fold_kernel, rank), jax.ShapeDtypeStruct(proj.shape, BF), proj)
    everyone = swap(proj)
    left, right, side, mine = late
    sent = reduce_3(left, right, side, up, down, other)
    got = to_dp(sent[0], 1, 0), to_dp(sent[1], -1, 0), to_dp(sent[2], 0, 1)
    own_pre = ((f(mine) + f(got[0])) + (f(got[1]) + f(got[2]))).astype(BF)

    left, right = to_dp(own_pre, 1, 0), to_dp(own_pre, -1, 0)
    part = call(first_kernel, tok, own_pre, everyone)
    got, _, mine = hop(part, 1, (own_pre,), lambda a: (a[:h], a[h:]))
    side_low = to_dp(mine[0], 0, 1)
    part = call(forward_kernel, tok, own_pre, everyone, *got)
    got, _, _ = hop(part, 1)
    got, left, right, side_low, high = tie(got, left, right, side_low, mine[1])
    side_high = to_dp(high, 0, 1)
    far_0, far_1 = to_dp(left[:h], 1, 0), to_dp(right[h:], -1, 0)
    part = call(forward_kernel, tok, own_pre, everyone, *got)
    got, _, _ = hop(part, 1)
    got, far_0, far_1 = tie(got, far_0, far_1)
    left_low, right_low = to_dp(side_low, 1, 0), to_dp(side_low, -1, 0)
    c_in, coef_part, slope = call(
        middle_kernel,
        (jax.ShapeDtypeStruct((own, rank), BF), tok, jax.ShapeDtypeStruct((own, hid), BF)),
        own_pre, everyone, *got,
    )
    cot = cotangent.reshape(own, rank)

    def back(got):
        return call(backward_kernel, tok, last, slope, everyone, cot, *got)

    got, _, _ = hop(back((cot, cot)), -1)
    got, side_high, left_low, right_low = tie(got, side_high, left_low, right_low)
    left_high, right_high = to_dp(side_high, 1, 0), to_dp(side_high, -1, 0)
    far_low = to_dp(left_low, 1, 0)
    got, _, _ = hop(back(got), -1)
    got, left_high, right_high = tie(got, left_high, right_high)
    far_high = to_dp(right_high, -1, 0)
    got, _, _ = hop(back(got), -1)
    got, far_low, far_high = tie(got, far_low, far_high)
    g_out = jnp.where(last[0] == 1, cot, got[0] + got[1])
    ex = jnp.concatenate([g_out.astype(BF), c_in], axis=1)
    ex = swap(jnp.broadcast_to(ex[None], (dp,) + ex.shape))
    parts = cat(coef_part, back(got))
    parts = parts + to_tensor(parts, 1)
    ex, parts = tie(ex, parts)
    pieces = [
        own_pre, side_low, side_high, left, left_low, left_high,
        right, right_low, right_high, far_0, far_1, far_low, far_high,
    ]
    grad_up, down_coefs = finish(place, ex, everyone, base_t, basis, pieces)
    parts = (parts + to_tensor(parts, 2)).reshape(2, 1, micro, rows, rank)
    return parts[0], parts[1], grad_up[None], down_coefs[None]


def solution(mesh):
    return jax.shard_map(
        on_device,
        mesh=mesh,
        in_specs=(
            P(None, None, "dp"),
            P("section", "dp", "tensor"),
            P("section", "tensor", "dp"),
            P("dp", None),
            P(None, "dp", None),
        ),
        out_specs=(
            P("section", None, "dp", None),
            P("section", None, "dp", None),
            P("section", "dp", "tensor"),
            P("section", "tensor", None),
        ),
        check_vma=False,
    )
```

```python
import functools

import jax
import jax.numpy as jnp
from jax import lax
from jax.experimental import pallas as pl
from jax.experimental.pallas import tpu as pltpu
from jax.sharding import PartitionSpec as P

BF = jnp.bfloat16
F32 = jnp.float32
HIGHEST = lax.Precision.HIGHEST
NT = (((1,), (1,)), ((), ()))
CHUNK = 512
WIDE_CHUNK = 1792
PROJ_CHUNK = 896
X_SIZE = 4
RELATIVE = ((0, 0), (0, 1), (-1, 0), (-1, 1), (1, 0), (1, 1), (2, 0), (2, 1))
EARLY, LATE = (7, 6, 3, 5), (2, 4, 1, 0)
PARAMS = pltpu.CompilerParams(vmem_limit_bytes=60 * 1024 * 1024)
SMALL = pltpu.CompilerParams(vmem_limit_bytes=16 * 1024 * 1024)


def split2(x):
    hi = x.astype(BF)
    return hi, (x - hi.astype(F32)).astype(BF)


def mm(a, b):
    return jnp.dot(a, b, preferred_element_type=F32)


def mm_nt(a, b):
    return lax.dot_general(a, b, NT, preferred_element_type=F32)


def sigma(v):
    return 0.5 * jnp.tanh(0.5 * v) + 0.5


def wide(x):
    return jnp.concatenate(split2(x), axis=1)


def tall(x):
    return jnp.concatenate(split2(x), axis=0)


def twice(x):
    return jnp.concatenate([x, x], axis=0)


def chunks_of(width):
    return [slice(i, i + CHUNK) for i in range(0, width, CHUNK)]


def up_of(all_ref, cols):
    dp, rows, _ = all_ref.shape
    return all_ref[:, : rows // 2, cols].reshape(dp * rows // 2, -1)


def down_of(all_ref, cols):
    dp, rows, _ = all_ref.shape
    return all_ref[:, rows // 2 :, cols].reshape(dp * rows // 2, -1)


def gram_share(x, all_ref):
    rank = x.shape[1]
    cols = slice(all_ref.shape[2] - rank, all_ref.shape[2])
    gram = up_of(all_ref, cols).astype(F32) + down_of(all_ref, cols).astype(F32)
    return 0.25 * jnp.dot(x, gram, precision=HIGHEST, preferred_element_type=F32)


def first_kernel(base_ref, all_ref, part_ref):
    acc = jnp.zeros(part_ref.shape, F32)
    for cols in chunks_of(base_ref.shape[1]):
        pre = base_ref[:, cols].astype(F32)
        hidden = (pre * sigma(pre)).astype(BF)
        acc += mm_nt(hidden, down_of(all_ref, cols))
    part_ref[...] = acc


def forward_kernel(base_ref, all_ref, r0, r1, part_ref):
    c = r0[...] + r1[...]
    cw = wide(c)
    acc = gram_share(c, all_ref)
    for cols in chunks_of(base_ref.shape[1]):
        pre = base_ref[:, cols].astype(F32) + mm(cw, twice(up_of(all_ref, cols)))
        hidden = (pre * sigma(pre)).astype(BF)
        acc += mm_nt(hidden, down_of(all_ref, cols))
    part_ref[...] = acc


def middle_kernel(base_ref, all_ref, r0, r1, c_ref, part_ref, slope_ref):
    c = r0[...] + r1[...]
    c_ref[...] = c.astype(BF)
    cw = wide(c)
    acc = gram_share(c, all_ref)
    for cols in chunks_of(base_ref.shape[1]):
        pre = base_ref[:, cols].astype(F32) + mm(cw, twice(up_of(all_ref, cols)))
        sig = sigma(pre)
        hidden = (pre * sig).astype(BF)
        slope_ref[:, cols] = (sig * (1.0 + pre * (1.0 - sig))).astype(BF)
        acc += mm_nt(hidden, down_of(all_ref, cols))
    part_ref[...] = acc


def backward_kernel(last_ref, slope_ref, all_ref, cot_ref, r0, r1, part_ref):
    g = jnp.where(last_ref[0] == 1, cot_ref[...], r0[...] + r1[...])
    gw = wide(g)
    acc = gram_share(g, all_ref)
    for cols in chunks_of(slope_ref.shape[1]):
        g_pre = mm(gw, twice(down_of(all_ref, cols))) * slope_ref[:, cols].astype(F32)
        acc += mm_nt(g_pre.astype(BF), up_of(all_ref, cols))
    part_ref[...] = acc


def call(kernel, outs, *args):
    return pl.pallas_call(kernel, out_shape=outs, compiler_params=SMALL)(*args)


def base_specs(base, dp, blocks):
    micro, tokens, width = base.shape
    return [
        pl.BlockSpec((micro, tokens // dp, width), lambda i, p, j=j: (0, p[j], 0)) for j in blocks
    ]


def product_kernel(count, plan, place_ref, *refs):
    bases, w_ref, outs, rows = refs[:count], refs[count], refs[count + 1 : -1], refs[-1]
    own = bases[0].shape[0] * bases[0].shape[1]

    @pl.when(pl.program_id(0) == 0)
    def _():
        for j, b in enumerate(bases):
            rows[j * own : (j + 1) * own] = b[...].reshape(own, b.shape[2])

    res = mm(rows[...], w_ref[...])
    for out, parts in zip(outs, plan):
        start = 0
        for j, begin, end in parts:
            out[start : start + end - begin] = res[j * own + begin : j * own + end].astype(BF)
            start += end - begin


def product(place, base, w_in, dp, blocks, plan):
    micro, tokens, width = base.shape
    hid = w_in.shape[1]
    own = micro * tokens // dp
    count = len(blocks)
    heights = [sum(end - begin for _, begin, end in parts) for parts in plan]
    column = lambda rows: pl.BlockSpec((rows, WIDE_CHUNK), lambda i, p: (0, i))
    return pl.pallas_call(
        functools.partial(product_kernel, count, plan),
        out_shape=[jax.ShapeDtypeStruct((rows, hid), BF) for rows in heights],
        grid_spec=pltpu.PrefetchScalarGridSpec(
            num_scalar_prefetch=1,
            grid=(hid // WIDE_CHUNK,),
            in_specs=base_specs(base, dp, blocks) + [column(width)],
            out_specs=[column(rows) for rows in heights],
            scratch_shapes=[pltpu.VMEM((own * count, width), BF)],
        ),
        compiler_params=PARAMS,
    )(place, *([base] * count), w_in)


def project_kernel(basis_ref, w_in_ref, w_out_ref, out_ref, wide_ref, tall_ref):
    rank = basis_ref.shape[1]
    count, rows, cols = out_ref.shape
    share = rows // 2
    step = pl.program_id(0)

    @pl.when(step == 0)
    def _():
        basis = basis_ref[...]
        wide_ref[...] = wide(basis)
        tall_ref[...] = tall(basis.T)
        gram = jnp.dot(basis.T, basis, precision=HIGHEST, preferred_element_type=F32)
        hi, lo = split2(gram)
        out_ref[:, :share, cols - rank :] = hi.reshape(count, share, rank)
        out_ref[:, share:, cols - rank :] = lo.reshape(count, share, rank)

    here = pl.ds(pl.multiple_of(step * PROJ_CHUNK, PROJ_CHUNK), PROJ_CHUNK)
    up = mm(tall_ref[...], w_in_ref[...])
    down = mm(w_out_ref[...], wide_ref[...])
    out_ref[:, :share, here] = (up[:rank] + up[rank:]).astype(BF).reshape(count, share, PROJ_CHUNK)
    down = (down[:, :rank] + down[:, rank:]).T
    out_ref[:, share:, here] = down.astype(BF).reshape(count, share, PROJ_CHUNK)


def project(basis, w_in, w_out, dp):
    width, rank = basis.shape
    hid = w_in.shape[1]
    shape = (dp, 2 * rank // dp, hid + rank)
    return pl.pallas_call(
        project_kernel,
        out_shape=jax.ShapeDtypeStruct(shape, BF),
        grid=(hid // PROJ_CHUNK,),
        in_specs=[
            pl.BlockSpec((width, rank), lambda i: (0, 0)),
            pl.BlockSpec((width, PROJ_CHUNK), lambda i: (0, i)),
            pl.BlockSpec((PROJ_CHUNK, width), lambda i: (i, 0)),
        ],
        out_specs=pl.BlockSpec(shape, lambda i: (0, 0, 0)),
        scratch_shapes=[pltpu.VMEM((width, 2 * rank), BF), pltpu.VMEM((2 * rank, width), BF)],
        compiler_params=PARAMS,
    )(basis, w_in, w_out)


def fold_kernel(rank, x_ref, out_ref):
    count, rows, cols = x_ref.shape
    share = rows // 2
    total = x_ref[0].astype(F32)
    for d in range(1, count):
        total += x_ref[d].astype(F32)
    hi, lo = split2(total[:share, cols - rank :] + total[share:, cols - rank :])
    own = jnp.concatenate(
        [total[:, : cols - rank].astype(BF), jnp.concatenate([hi, lo], axis=0)], axis=1
    )
    for d in range(count):
        out_ref[d] = own


def turn_kernel(place_ref, *refs):
    bases, out = refs[:-1], refs[-1]
    own = bases[0].shape[0] * bases[0].shape[1]
    for j, b in enumerate(bases):
        rows = b[...].reshape(own, b.shape[2]).astype(F32)
        out[:, j * own : (j + 1) * own] = rows.T.astype(BF)


def turn(place, base, dp):
    micro, tokens, width = base.shape
    count = len(RELATIVE)
    shape = (width, micro * tokens)
    return pl.pallas_call(
        turn_kernel,
        out_shape=jax.ShapeDtypeStruct(shape, BF),
        grid_spec=pltpu.PrefetchScalarGridSpec(
            num_scalar_prefetch=1,
            grid=(1,),
            in_specs=base_specs(base, dp, range(count)),
            out_specs=pl.BlockSpec(shape, lambda i, p: (0, 0)),
        ),
        compiler_params=PARAMS,
    )(place, *([base] * count))


def finish_kernel(place_ref, ex_ref, all_ref, base_ref, basis_ref, *refs):
    pieces, (grad_ref, dc_ref, xt, gg, gt, cc, hidden, g_pre) = refs[:-8], refs[-8:]
    own, two = ex_ref.shape[1:]
    rank = two // 2

    @pl.when(pl.program_id(0) == 0)
    def _():
        basis = basis_ref[...].astype(BF)
        for j in range(len(RELATIVE)):
            ex = ex_ref[place_ref[j]]
            rows = slice(j * own, (j + 1) * own)
            g, c = ex[:, :rank], ex[:, rank:]
            gg[rows] = g
            cc[rows] = c
            gt[:, rows] = g.astype(F32).T.astype(BF)
            xt[:, rows] = (base_ref[:, rows].astype(F32) + mm_nt(basis, c)).astype(BF)

    every = slice(0, all_ref.shape[2])
    from_c = mm(cc[...], up_of(all_ref, every))
    g_hidden = mm(gg[...], down_of(all_ref, every))
    start = 0
    for p in pieces:
        rows = slice(start, start + p.shape[0])
        start += p.shape[0]
        pre = p[...].astype(F32) + from_c[rows]
        sig = sigma(pre)
        out = pre * sig
        hidden[rows] = out.astype(BF)
        g_pre[rows] = (g_hidden[rows] * (sig + out * (1.0 - sig))).astype(BF)
    grad_ref[...] = mm(xt[...], g_pre[...]).astype(BF)
    dc_ref[...] = mm(gt[...], hidden[...]).T


def finish(place, ex, everyone, base_t, basis, pieces):
    width, tokens = base_t.shape
    hid = pieces[0].shape[1]
    rank = basis.shape[1]
    dp, rows, _ = everyone.shape
    column = lambda rows: pl.BlockSpec((rows, CHUNK), lambda i, p: (0, i))
    return pl.pallas_call(
        finish_kernel,
        out_shape=[jax.ShapeDtypeStruct((width, hid), BF), jax.ShapeDtypeStruct((hid, rank), F32)],
        grid_spec=pltpu.PrefetchScalarGridSpec(
            num_scalar_prefetch=1,
            grid=(hid // CHUNK,),
            in_specs=[
                pl.BlockSpec(ex.shape, lambda i, p: (0, 0, 0)),
                pl.BlockSpec((dp, rows, CHUNK), lambda i, p: (0, 0, i)),
                pl.BlockSpec(base_t.shape, lambda i, p: (0, 0)),
                pl.BlockSpec(basis.shape, lambda i, p: (0, 0)),
            ]
            + [column(p.shape[0]) for p in pieces],
            out_specs=[column(width), pl.BlockSpec((CHUNK, rank), lambda i, p: (i, 0))],
            scratch_shapes=[
                pltpu.VMEM((width, tokens), BF),
                pltpu.VMEM((tokens, rank), BF),
                pltpu.VMEM((rank, tokens), BF),
                pltpu.VMEM((tokens, rank), BF),
                pltpu.VMEM((tokens, CHUNK), BF),
                pltpu.VMEM((tokens, CHUNK), BF),
            ],
        ),
        compiler_params=PARAMS,
    )(place, ex, everyone, base_t, basis, *pieces)


def to_dp(x, dx, dy):
    size = lax.axis_size("dp")
    pairs = [(i, ((i // 2 + dx) % X_SIZE) * 2 + ((i % 2) ^ dy)) for i in range(size)]
    return lax.ppermute(x, "dp", pairs)


def to_tensor(x, k):
    size = lax.axis_size("tensor")
    return lax.ppermute(x, "tensor", [(t, t ^ k) for t in range(size)])


def hop(part, by, before=(), during=lambda *a: ()):
    sections, tensors = lax.axis_size("section"), lax.axis_size("tensor")
    pair_sum, before = tie(part + to_tensor(part, 1), before)
    pairs = [
        (s * tensors + t, (s + by) * tensors + (t ^ (2 * (t % 2))))
        for s in range(sections)
        for t in range(tensors)
        if 0 <= s + by < sections
    ]
    got = lax.ppermute(pair_sum, ("section", "tensor"), pairs)
    got, made = tie(got, during(*before))
    return (got, to_tensor(got, 1)), before, made


def cat(*xs):
    return jnp.concatenate(xs, axis=0)


def plus(x, *ys):
    total = x.astype(F32)
    for start, y in ys:
        pads = ((start, x.shape[0] - start - y.shape[0]), (0, 0))
        total = total + jnp.pad(y.astype(F32), pads)
    return total.astype(x.dtype)


def reduce_2(two, left_1, right_1, steps):
    u0, u1, v = steps
    h, q = two.shape[0] // 2, two.shape[0] // 4
    up = cat(two[:h], plus(right_1, (0, u0)))
    down = cat(plus(two[h:], (0, v)), plus(left_1, (q, u1)))
    return up, down


def reduce_3(left, right, side, up, down, other):
    h = left.shape[0] // 2
    return (
        plus(right, (0, up[:h]), (h, other[:h])),
        plus(left, (h, down[:h]), (h, other[h:])),
        plus(side, (0, up[h:]), (0, down[h:])),
    )


def swap(x):
    return lax.all_to_all(x, "dp", 0, 0, tiled=True)


def tie(*xs):
    return lax.optimization_barrier(xs)


def on_device(base, w_in, w_out, basis, cotangent):
    dp = lax.axis_size("dp")
    sections = lax.axis_size("section")
    last = (lax.axis_index("section") == sections - 1).astype(jnp.int32).reshape(1)
    d = lax.axis_index("dp")
    place = jnp.stack(
        [((d // 2 + dx) % X_SIZE) * 2 + (d % 2 + dy) % 2 for dx, dy in RELATIVE]
    ).astype(jnp.int32)
    micro, tokens, width = base.shape
    rows = tokens // dp
    own = micro * rows
    rank = basis.shape[1]
    w_in, w_out = w_in[0], w_out[0]
    hid = w_in.shape[1]
    tok = jax.ShapeDtypeStruct((own, rank), F32)
    f = lambda a: a.astype(F32)

    h, q = own // 2, own // 4
    cuts = [
        [(0, 0, q)], [(0, q, h)], [(0, h, own)], [(1, 0, own)], [(2, 0, h)], [(3, 0, h)],
        [(3, h, own), (2, h, own)],
    ]
    early = product(place, base, w_in, dp, EARLY, cuts)
    (*far, two, left_1, right_1, other), base_1 = tie(early, base)
    steps = to_dp(far[0], 1, 0), to_dp(far[1], -1, 0), to_dp(far[2], 0, 1)
    base_t = turn(place, base_1, dp)
    steps, base_t = tie(steps, base_t)
    up, down = reduce_2(two, left_1, right_1, steps)
    up, down, basis_1 = tie(up, down, basis)
    up, down, other = to_dp(up, 1, 0), to_dp(down, -1, 0), to_dp(other, 0, 1)
    proj = project(basis_1, w_in, w_out, dp)
    up, down, base_2 = tie(up, down, base_1)
    proj = swap(proj)
    late = product(place, base_2, w_in, dp, LATE, [[(j, 0, own)] for j in range(len(LATE))])
    proj = call(functools.partial(fold_kernel, rank), jax.ShapeDtypeStruct(proj.shape, BF), proj)
    everyone = swap(proj)
    left, right, side, mine = late
    sent = reduce_3(left, right, side, up, down, other)
    got = to_dp(sent[0], 1, 0), to_dp(sent[1], -1, 0), to_dp(sent[2], 0, 1)
    own_pre = ((f(mine) + f(got[0])) + (f(got[1]) + f(got[2]))).astype(BF)

    left, right = to_dp(own_pre, 1, 0), to_dp(own_pre, -1, 0)
    part = call(first_kernel, tok, own_pre, everyone)
    got, _, mine = hop(part, 1, (own_pre,), lambda a: (a[:h], a[h:]))
    side_low = to_dp(mine[0], 0, 1)
    part = call(forward_kernel, tok, own_pre, everyone, *got)
    got, _, _ = hop(part, 1)
    got, left, right, side_low, high = tie(got, left, right, side_low, mine[1])
    side_high = to_dp(high, 0, 1)
    far_0, far_1 = to_dp(left[:h], 1, 0), to_dp(right[h:], -1, 0)
    part = call(forward_kernel, tok, own_pre, everyone, *got)
    got, _, _ = hop(part, 1)
    got, far_0, far_1 = tie(got, far_0, far_1)
    left_low, right_low = to_dp(side_low, 1, 0), to_dp(side_low, -1, 0)
    c_in, coef_part, slope = call(
        middle_kernel,
        (jax.ShapeDtypeStruct((own, rank), BF), tok, jax.ShapeDtypeStruct((own, hid), BF)),
        own_pre, everyone, *got,
    )
    cot = cotangent.reshape(own, rank)

    def back(got):
        return call(backward_kernel, tok, last, slope, everyone, cot, *got)

    got, _, _ = hop(back((cot, cot)), -1)
    got, side_high, left_low, right_low = tie(got, side_high, left_low, right_low)
    left_high, right_high = to_dp(side_high, 1, 0), to_dp(side_high, -1, 0)
    far_low = to_dp(left_low, 1, 0)
    got, _, _ = hop(back(got), -1)
    got, left_high, right_high = tie(got, left_high, right_high)
    far_high = to_dp(right_high, -1, 0)
    got, _, _ = hop(back(got), -1)
    got, far_low, far_high = tie(got, far_low, far_high)
    g_out = jnp.where(last[0] == 1, cot, got[0] + got[1])
    ex = jnp.concatenate([g_out.astype(BF), c_in], axis=1)
    ex = swap(jnp.broadcast_to(ex[None], (dp,) + ex.shape))
    parts = cat(coef_part, back(got))
    parts = parts + to_tensor(parts, 1)
    ex, parts = tie(ex, parts)
    pieces = [
        own_pre, side_low, side_high, left, left_low, left_high,
        right, right_low, right_high, far_0, far_1, far_low, far_high,
    ]
    grad_up, down_coefs = finish(place, ex, everyone, base_t, basis, pieces)
    parts = (parts + to_tensor(parts, 2)).reshape(2, 1, micro, rows, rank)
    return parts[0], parts[1], grad_up[None], down_coefs[None]


def solution(mesh):
    return jax.shard_map(
        on_device,
        mesh=mesh,
        in_specs=(
            P(None, None, "dp"),
            P("section", "dp", "tensor"),
            P("section", "tensor", "dp"),
            P("dp", None),
            P(None, "dp", None),
        ),
        out_specs=(
            P("section", None, "dp", None),
            P("section", None, "dp", None),
            P("section", "dp", "tensor"),
            P("section", "tensor", None),
        ),
        check_vma=False,
    )
```
